128 devices in a mesh: dp: 16 (over z, x_hi, core), sub: 8 (over x_lo, y).
Axes of the slice: x: 4 (x_hi: 2, x_lo: 2; x = x_hi * 2 + x_lo), y: 4, z: 4, core: 2. Of those that a mesh axis runs over, the one named last changes fastest.
Arguments:
- tokens: bfloat16 [16384, 768], P(('dp', 'sub')), may hold values from -6 to 6
- cotangent: bfloat16 [16384, 768], P(('dp', 'sub')), may hold values from -6 to 6
- seq_lengths: int32 [128, 4], P(('dp', 'sub')), may hold values from 0 to 128, as said below
- norm_gain: bfloat16 [768], P(('dp', 'sub')), may hold values from 0.5 to 1.5
- weight_query: bfloat16 [768, 768], P(('dp', 'sub')), may hold values from -0.21875 to 0.21875
- weight_key: bfloat16 [768, 768], P(('dp', 'sub')), may hold values from -0.21875 to 0.21875
- weight_value: bfloat16 [768, 768], P(('dp', 'sub')), may hold values from -0.21875 to 0.21875
- weight_rate: bfloat16 [768, 12], P(('dp', 'sub')), may hold values from -0.21875 to 0.21875
- bias_rate: bfloat16 [12], replicated, may hold values from -3 to 3
- init_weight: bfloat16 [768, 64], P(('dp', 'sub')), may hold values from -0.75 to 0.75
- init_bias: bfloat16 [768], P(('dp', 'sub')), may hold values from -3 to 3
- inner_gain: bfloat16 [768], P(('dp', 'sub')), may hold values from 0.5 to 1.5
- inner_bias: bfloat16 [768], P(('dp', 'sub')), may hold values from -3 to 3
- post_gain: bfloat16 [768], P(('dp', 'sub')), may hold values from 0.5 to 1.5
- post_bias: bfloat16 [768], P(('dp', 'sub')), may hold values from -3 to 3
- weight_out: bfloat16 [768, 768], P(('dp', 'sub')), may hold values from -0.21875 to 0.21875
- mlp_gain: bfloat16 [768], P(('dp', 'sub')), may hold values from 0.5 to 1.5
- weight_gate: bfloat16 [768, 2048], P(('dp', 'sub')), may hold values from -0.21875 to 0.21875
- weight_up: bfloat16 [768, 2048], P(('dp', 'sub')), may hold values from -0.21875 to 0.21875
- weight_down: bfloat16 [768, 2048], P(('dp', 'sub')), may hold values from -0.125 to 0.125
Outputs:
- output: bfloat16 [16384, 768], P(('dp', 'sub'))
- grad_tokens: bfloat16 [16384, 768], P(('dp', 'sub'))
- grad_norm_gain: float32 [768], P(('dp', 'sub'))
- grad_query: float32 [768, 768], P(('dp', 'sub'))
- grad_key: float32 [768, 768], P(('dp', 'sub'))
- grad_value: float32 [768, 768], P(('dp', 'sub'))
- grad_rate: float32 [768, 12], P(('dp', 'sub'))
- grad_bias_rate: float32 [12], replicated
- grad_init_weight: float32 [768, 64], P(('dp', 'sub'))
- grad_init_bias: float32 [768], P(('dp', 'sub'))
- grad_inner_gain: float32 [768], P(('dp', 'sub'))
- grad_inner_bias: float32 [768], P(('dp', 'sub'))
- grad_post_gain: float32 [768], P(('dp', 'sub'))
- grad_post_bias: float32 [768], P(('dp', 'sub'))
- grad_out: float32 [768, 768], P(('dp', 'sub'))
- grad_mlp_gain: float32 [768], P(('dp', 'sub'))
- grad_gate: float32 [768, 2048], P(('dp', 'sub'))
- grad_up: float32 [768, 2048], P(('dp', 'sub'))
- grad_down: float32 [768, 2048], P(('dp', 'sub'))
- rate_mean: float32 [], replicated
- rate_max: float32 [], replicated
The draws below stay inside these ranges and needn't reach their ends.
Inputs may be any that keep to these rules, and one draw needn't show every extreme that they name: `seq_lengths`: row d lists, in order, the sequences packed into the 128 slots of device d (devices in dp-major order); each takes its length rounded up to a multiple of 16 slots, right after the previous one; a length of 0 takes no slots and the rounded lengths of a row sum to at most 128; the first length of every row is 1 or more; in every draw one device holds a single sequence of exactly 128 tokens.
All inputs are finite; a program needn't handle non-finite values.
Results may differ from the reference program's by a relative error of at most 0.0081.
Values may be sent and summed in bfloat16 or wider, within the bound.
A program may use at most 192 MiB of HBM per device.

```python
import jax
import jax.numpy as jnp
from jax import lax

HEADS = 12
HEAD = 64
D = 768
FF = 2048
MINI = 16
SEQ_DEV = 4
TOK_DEV = 128
TOKENS = 16384
N_DP = 16
N_SUB = 8


def draw_seq_lengths(key, part):
    key = jax.random.fold_in(key, 7)
    key_a, key_b, key_c = jax.random.split(key, 3)
    device_total = N_DP * N_SUB
    top_blocks = TOK_DEV // MINI // SEQ_DEV
    device_ids = jnp.arange(device_total, dtype=jnp.int32)
    low_blocks = 1 + (top_blocks - 1) * device_ids // max(device_total - 1, 1)
    span_blocks = top_blocks - low_blocks + 1
    uniform_bits = jax.random.randint(key_a, (device_total, SEQ_DEV), 0, 1 << 20)
    blocks = low_blocks[:, None] + uniform_bits % span_blocks[:, None]
    trim_tokens = jax.random.randint(key_b, (device_total, SEQ_DEV), 0, MINI)
    lengths = blocks * MINI - trim_tokens
    chosen = jax.random.randint(key_c, (), 0, device_total)
    whole_row = jnp.where(jnp.arange(SEQ_DEV, dtype=jnp.int32) == 0, TOK_DEV, 0).astype(jnp.int32)
    lengths = jnp.where((device_ids == chosen)[:, None], whole_row[None, :], lengths)
    return lengths.astype(jnp.int32)


def shard_levels(key, shape, pieces, low, largest):
    def one(position, parts):
        steps = jax.random.uniform(jax.random.fold_in(jax.random.fold_in(key, 6), position), (parts,), jnp.float32, low / len(pieces), largest / len(pieces))
        return jnp.repeat(jnp.exp(steps), shape[position] // parts).reshape((-1,) + (1,) * (len(shape) - position - 1))

    gain = one(*pieces[0])
    for cut in pieces[1:]:
        gain = gain * one(*cut)
    return gain


def bell_draw(own_key, extent, scale, bound, pieces=(), held_as=jnp.bfloat16):
    factor_of = shard_levels(own_key, extent, pieces, -0.22, 0.18) if pieces else 1.0
    array = jax.random.normal(own_key, extent, jnp.float32) * scale * factor_of
    return jnp.minimum(jnp.maximum(array, -bound), bound).astype(held_as)


def setup_inputs(seed: int = 0) -> dict:
    streams_of = jax.random.split(jax.random.key(seed), 21)
    return {
        "tokens": bell_draw(streams_of[0], (TOKENS, D), 1.0, 6.0, ((0, 128),)),
        "cotangent": bell_draw(streams_of[1], (TOKENS, D), 1.0, 6.0, ((0, 128),)),
        "seq_lengths": draw_seq_lengths(jax.random.fold_in(streams_of[20], 71), 0),
        "norm_gain": jnp.clip(1.0 + 0.1 * jax.random.normal(streams_of[3], (D,), jnp.float32), 0.5, 1.5).astype(jnp.bfloat16),
        "weight_query": bell_draw(streams_of[4], (D, D), D ** -0.5, 0.21875, ((0, 128),)),
        "weight_key": bell_draw(streams_of[5], (D, D), D ** -0.5, 0.21875, ((0, 128),)),
        "weight_value": bell_draw(streams_of[6], (D, D), D ** -0.5, 0.21875, ((0, 128),)),
        "weight_rate": bell_draw(streams_of[7], (D, HEADS), D ** -0.5, 0.21875, ((0, 128),)),
        "bias_rate": bell_draw(streams_of[8], (HEADS,), 1.0, 3.0),
        "init_weight": bell_draw(streams_of[9], (D, HEAD), HEAD ** -0.5, 0.75, ((0, 128),)),
        "init_bias": bell_draw(streams_of[10], (D,), 0.5, 3.0, ((0, 128),)),
        "inner_gain": jnp.clip(1.0 + 0.1 * jax.random.normal(streams_of[11], (D,), jnp.float32), 0.5, 1.5).astype(jnp.bfloat16),
        "inner_bias": bell_draw(streams_of[12], (D,), 0.5, 3.0, ((0, 128),)),
        "post_gain": jnp.clip(1.0 + 0.1 * jax.random.normal(streams_of[13], (D,), jnp.float32), 0.5, 1.5).astype(jnp.bfloat16),
        "post_bias": bell_draw(streams_of[14], (D,), 0.5, 3.0, ((0, 128),)),
        "weight_out": bell_draw(streams_of[15], (D, D), D ** -0.5, 0.21875, ((0, 128),)),
        "mlp_gain": jnp.clip(1.0 + 0.1 * jax.random.normal(streams_of[16], (D,), jnp.float32), 0.5, 1.5).astype(jnp.bfloat16),
        "weight_gate": bell_draw(streams_of[17], (D, FF), D ** -0.5, 0.21875, ((0, 128),)),
        "weight_up": bell_draw(streams_of[18], (D, FF), D ** -0.5, 0.21875, ((0, 128),)),
        "weight_down": bell_draw(streams_of[19], (D, FF), FF ** -0.5, 0.125, ((0, 128),)),
    }


EPS = 1e-06
BASE_RATE = 1.0

@jax.custom_vjp
def low(v):
    return lax.optimization_barrier(v.astype(jnp.bfloat16)).astype(jnp.float32)

@jax.custom_vjp
def low_back(v):
    return v

def low_keep(v):
    return (low(v), None)

def low_pass(kept, grad):
    return (grad,)

def back_keep(v):
    return (v, None)

def back_low(kept, grad):
    return (low(grad),)
low.defvjp(low_keep, low_pass)
low_back.defvjp(back_keep, back_low)

def slot_layout(lengths, slot_total):
    lengths = lengths.astype(jnp.int32)
    padded = ((lengths + (MINI - 1)) // MINI * MINI).astype(jnp.int32)
    sequence_stops = jnp.cumsum(padded).astype(jnp.int32)
    seq_starts = (sequence_stops - padded).astype(jnp.int32)
    slot_ids = jnp.arange(slot_total, dtype=jnp.int32)
    inside = (slot_ids[:, None] >= seq_starts[None, :]) & (slot_ids[:, None] < seq_starts[None, :] + lengths[None, :])
    slot_mask = lax.optimization_barrier(jnp.max(inside.astype(jnp.float32), axis=1))
    batch_first = jnp.arange(slot_total // MINI, dtype=jnp.int32) * MINI
    opening = (batch_first[:, None] == seq_starts[None, :]) & (lengths[None, :] > 0)
    batch_open = lax.optimization_barrier(jnp.max(opening.astype(jnp.float32), axis=1))
    return (slot_mask, batch_open)

def head_norm(values, gain_vec, bias_vec):
    centre = values - lax.optimization_barrier(jnp.mean(values, axis=-1, keepdims=True))
    scaled = lax.rsqrt(lax.optimization_barrier(jnp.mean(centre * centre, axis=-1, keepdims=True)) + EPS)
    normed = centre * scaled
    return (normed * gain_vec + bias_vec, normed, scaled)

def inner_mixer(queries, key_rows, value_rows, rate_logit, slot_mask, batch_open, init_weight, init_bias, inner_gain, inner_bias):
    slot_total = queries.shape[0]
    batches = slot_total // MINI

    def heads_first(values):
        return values.reshape(batches, MINI, HEADS, HEAD).transpose(0, 2, 1, 3)
    rates = BASE_RATE / HEAD * jax.nn.sigmoid(rate_logit)
    rates = rates.reshape(batches, MINI, HEADS).transpose(0, 2, 1)
    weight_zero = init_weight.reshape(HEADS, HEAD, HEAD)
    bias_zero = init_bias.reshape(HEADS, HEAD)
    gain_heads = inner_gain.reshape(HEADS, 1, HEAD)
    shift_heads = inner_bias.reshape(HEADS, 1, HEAD)
    places = jnp.arange(MINI, dtype=jnp.float32)
    causal = (places[:, None] >= places[None, :]).astype(jnp.float32) / (places[:, None] + 1.0)
    precise_result = lax.Precision.HIGHEST

    def advance(carried, inputs_mb):
        current_weight, current_bias = carried
        query_mb, key_minibatch, value_mb, rate_mb, mask_mb, opening = inputs_mb
        current_weight = opening * weight_zero + (1.0 - opening) * current_weight
        current_bias = opening * bias_zero + (1.0 - opening) * current_bias
        inner_preactivation = jnp.einsum('svf,sfl->svl', key_minibatch, current_weight, precision=precise_result) + current_bias[:, None, :]
        rebuilt, normed, scaled = head_norm(inner_preactivation, gain_heads, shift_heads)
        error_term = gain_heads * (rebuilt - (value_mb - key_minibatch))
        grad_pre = scaled * (error_term - lax.optimization_barrier(jnp.mean(error_term, axis=-1, keepdims=True)) - normed * lax.optimization_barrier(jnp.mean(error_term * normed, axis=-1, keepdims=True)))
        grad_pre = grad_pre * mask_mb[None, :, None]
        step_rates = causal[None] * rate_mb[:, None, :]
        scores = jnp.einsum('hid,hjd->hij', query_mb, key_minibatch, precision=precise_result) + 1.0
        updated = jnp.einsum('hid,hde->hie', query_mb, current_weight, precision=precise_result) + current_bias[:, None, :] - jnp.einsum('hij,hje->hie', step_rates * scores, grad_pre, precision=precise_result)
        answer, unused_a, unused_b = head_norm(updated, gain_heads, shift_heads)
        last_rates = rate_mb / MINI
        weight_next = current_weight - jnp.einsum('hjd,hje->hde', key_minibatch * last_rates[:, :, None], grad_pre, precision=precise_result)
        bias_next = current_bias - lax.optimization_barrier(jnp.sum(last_rates[:, :, None] * grad_pre, axis=1))
        return ((weight_next, bias_next), query_mb + answer)
    initial = (jnp.zeros((HEADS, HEAD, HEAD), jnp.float32), jnp.zeros((HEADS, HEAD), jnp.float32))
    unused_state, outputs = lax.scan(advance, initial, (heads_first(queries), heads_first(key_rows), heads_first(value_rows), rates, slot_mask.reshape(batches, MINI), batch_open))
    return outputs.transpose(0, 2, 1, 3).reshape(slot_total, HEADS * HEAD)

def rms_scale(values):
    return lax.rsqrt(lax.optimization_barrier(jnp.mean(values * values, axis=-1, keepdims=True)) + EPS)

def row_norm(values):
    centre = values - lax.optimization_barrier(jnp.mean(values, axis=-1, keepdims=True))
    scaled = lax.rsqrt(lax.optimization_barrier(jnp.mean(centre * centre, axis=-1, keepdims=True)) + EPS)
    return (centre * scaled, scaled)

def matmul(left, right):
    return jnp.dot(left, right, precision=lax.Precision.HIGHEST)

def block(inputs, slot_mask, batch_open, params):
    norm_gain, weight_query, weight_key, weight_value, weight_rate, bias_rate, init_weight, init_bias, inner_gain, inner_bias, post_gain, post_bias, weight_out, mlp_gain, weight_gate, weight_up, weight_down = params
    normed = low(inputs * rms_scale(inputs) * norm_gain)
    queries = low_back(matmul(normed, weight_query))
    key_rows = low_back(matmul(normed, weight_key))
    value_rows = low_back(matmul(normed, weight_value))
    rate_logit = low_back(matmul(normed, weight_rate) + bias_rate)
    mixed = inner_mixer(queries, key_rows, value_rows, rate_logit, slot_mask, batch_open, init_weight, init_bias, inner_gain, inner_bias)
    post_hat, unused_scale = row_norm(mixed)
    post = low(post_hat * post_gain + post_bias)
    branch = low_back(matmul(post, weight_out))
    hidden = inputs + branch
    normed_two = low(hidden * rms_scale(hidden) * mlp_gain)
    gate = low_back(matmul(normed_two, weight_gate))
    up_proj = low_back(matmul(normed_two, weight_up))
    activ = low(jax.nn.silu(gate) * up_proj)
    mlp_out = low_back(matmul(activ, weight_down.T))
    rates = BASE_RATE / HEAD * jax.nn.sigmoid(rate_logit)
    return (slot_mask[:, None] * (hidden + mlp_out), rates)

def reference(tokens, cotangent, seq_lengths, norm_gain, weight_query, weight_key, weight_value, weight_rate, bias_rate, init_weight, init_bias, inner_gain, inner_bias, post_gain, post_bias, weight_out, mlp_gain, weight_gate, weight_up, weight_down):
    number_of_slabs = N_DP * N_SUB
    params = tuple((value.astype(jnp.float32) for value in (norm_gain, weight_query, weight_key, weight_value, weight_rate, bias_rate, init_weight, init_bias, inner_gain, inner_bias, post_gain, post_bias, weight_out, mlp_gain, weight_gate, weight_up, weight_down)))
    slabs = tokens.astype(jnp.float32).reshape(number_of_slabs, TOK_DEV, D)
    cot_slabs = cotangent.astype(jnp.float32).reshape(number_of_slabs, TOK_DEV, D)
    masks, opens = jax.vmap(lambda lengths: slot_layout(lengths, TOK_DEV))(seq_lengths)

    def forward(slab_in, weights_in):

        def one_slab(carried, inputs_slab):
            result, rates = jax.checkpoint(block)(inputs_slab[0], inputs_slab[1], inputs_slab[2], weights_in)
            return (carried, (result, rates))
        unused_carry, (results, rates) = lax.scan(one_slab, jnp.zeros((), jnp.float32), (slab_in, masks, opens))
        return (results, rates)
    results, pull_back, rates = jax.vjp(forward, slabs, params, has_aux=True)
    grad_in, grads = pull_back(cot_slabs)
    live_rates = masks[:, :, None] * rates
    rate_mean = jnp.sum(live_rates) / (jnp.sum(masks) * HEADS)
    rate_max = jnp.max(live_rates)
    return (results.reshape(TOKENS, D).astype(jnp.bfloat16), grad_in.reshape(TOKENS, D).astype(jnp.bfloat16), grads[0], grads[1], grads[2], grads[3], grads[4], grads[5], grads[6], grads[7], grads[8], grads[9], grads[10], grads[11], grads[12], grads[13], grads[14], grads[15], grads[16], rate_mean, rate_max)
```

```python
import jax
import jax.numpy as jnp
from jax import lax
from jax.experimental import pallas as pl
from jax.experimental.pallas import tpu as pltpu
from jax.sharding import PartitionSpec as P

MESH = pl.DeviceIdType.MESH
HEADS = 12
HEAD = 64
MINI = 16
EPS = 1e-06
F32 = jnp.float32
BF16 = jnp.bfloat16
S = 128
D = 768
FF = 2048
GROUPS = 3
RATE0 = 64
VEC0 = 76
ALL = slice(None)


class Wave:
    def __init__(self, base, nx, nz, ny, split=False):
        self.base, self.nx, self.nz, self.ny = base, nx, nz, ny
        self.half = 2 * nx + 2 * nz + 8 * ny
        self.per = nx + nz + ny
        self.split = split

    def start(self, h):
        return self.base if self.split else self.base + h * self.half

    def tx(self, h, xl):
        return self.start(h) + xl * self.nx

    def tz(self, h, xl):
        return self.start(h) + 2 * self.nx + xl * self.nz

    def ty(self, h, y, xl):
        return self.start(h) + 2 * self.nx + 2 * self.nz + (y * 2 + xl) * self.ny

    def mine(self, h, xl, y):
        return (
            [self.tx(h, xl) + n for n in range(self.nx)]
            + [self.tz(h, xl) + n for n in range(self.nz)]
            + [self.ty(h, y, xl) + n for n in range(self.ny)]
        )

    def span(self, color):
        return {
            "x": (0, 2 * self.nx),
            "z": (2 * self.nx, 2 * self.nz),
            "y": (2 * self.nx + 2 * self.nz, 8 * self.ny),
        }[color]

    def chain(self, color, me):
        if color == "x":
            return [
                ("z", lambda p: (self.tx(me.c, me.xl), self.nx, p, me.xh)),
                ("x", lambda p: (self.tx(me.c, p % 2), self.nx, ALL, p // 2)),
            ]
        if color == "z":
            return [
                ("x", lambda p: (self.tz(me.c, p % 2), self.nz, me.z, p // 2)),
                ("z", lambda p: (self.tz(me.c, 0), 2 * self.nz, p, ALL)),
            ]
        return [
            ("z", lambda p: (self.ty(me.c, me.y, me.xl), self.ny, p, me.xh)),
            ("x", lambda p: (self.ty(me.c, me.y, p % 2), self.ny, ALL, p // 2)),
            ("y", lambda p: (self.ty(me.c, p, 0), 2 * self.ny, ALL, ALL)),
        ]

    def colors(self, order="xzy"):
        return [k for k in order if {"x": self.nx, "z": self.nz, "y": self.ny}[k]]


ONE, THREE, TWO = Wave(0, 3, 3, 0), Wave(24, 1, 0, 0), Wave(28, 4, 4, 1, split=True)
OUT_WAVES = (ONE, THREE, TWO)
LAST, MID, FIRST = Wave(0, 2, 2, 0), Wave(16, 2, 1, 0), Wave(28, 4, 4, 1, split=True)
BACK_WAVES = (LAST, MID, FIRST)
TILES = 52
PER = max(sum(w.per for w in ws) for ws in (OUT_WAVES, BACK_WAVES))
PROWS = (PER * 6 + 15) // 16 * 16
TQ, TK, TS, TV = 0, 6, 12, 16
PADS = (25, 26, 27)
A_Q, A_K, A_V, A_O, A_G, A_U, A_D, A_S = range(8)
WIDTHS = (768, 768, 768, 768, 2048, 2048, 2048, 128)


def tile_out(c):
    return 13 + c if c < 3 else 19 + c


def tile_mlp(j, kind):
    return TWO.base + 6 * j + 2 * kind


def tile_source(w, h, t):
    if w.split:
        o = t - w.base
        return A_G + o % 6 // 2, 8 * h + o // 6 * 2 + o % 2
    if t in PADS:
        return None
    for a, first in ((A_Q, TQ), (A_K, TK), (A_V, TV)):
        if first <= t < first + 6:
            return a, t - first
    if t == TS:
        return A_S, 0
    return A_O, t - 13 if t < TV else t - 19


def nn(a, b):
    return lax.dot_general(a, b, (((1,), (0,)), ((), ())), preferred_element_type=F32)


def nt(a, b):
    return lax.dot_general(a, b, (((1,), (1,)), ((), ())), preferred_element_type=F32)


def tn(a, b):
    return lax.dot_general(a, b, (((0,), (0,)), ((), ())), preferred_element_type=F32)


def tt(a, b):
    return lax.dot_general(a, b, (((0,), (1,)), ((), ())), preferred_element_type=F32)


def iota(shape, dim):
    return lax.broadcasted_iota(jnp.int32, shape, dim)


def one_hot(cond):
    return jnp.where(cond, 1.0, 0.0).astype(BF16)


def split2(x):
    hi = x.astype(BF16)
    return hi, (x - hi.astype(F32)).astype(BF16)


def head_select(x, h):
    return jnp.where(iota(x.shape, 1) // HEAD == h, x, jnp.zeros_like(x))


def block_rows(x):
    return jnp.concatenate([head_select(x, h) for h in range(4)], axis=0)


def lanes(g):
    return pl.ds(256 * g, 256)


def layout_rows(lens_ref, token):
    mask = jnp.zeros(token.shape, F32)
    seg = jnp.zeros(token.shape, F32)
    start = jnp.int32(0)
    for j in range(4):
        n = lens_ref[0, j]
        mask += jnp.where((token >= start) & (token < start + n), 1.0, 0.0)
        seg += jnp.where((token >= start) & (n > 0), 1.0, 0.0)
        start += (n + 15) // 16 * 16
    return mask, seg


class Place:
    def __init__(self):
        dp, sub = lax.axis_index("dp"), lax.axis_index("sub")
        self.z = dp // 4
        self.xh = dp // 2 % 2
        self.c = dp % 2
        self.xl = sub // 4
        self.y = sub % 4
        self.x = self.xh * 2 + self.xl
        self.s = self.c * 8 + sub
        self.zx = self.z * 2 + self.xh

    def dev(self, z=None, x=None, y=None, c=None):
        z = self.z if z is None else z
        x = self.x if x is None else x
        y = self.y if y is None else y
        c = self.c if c is None else c
        return (z * 4 + x // 2 * 2 + c, x % 2 * 4 + y)

    def coord(self, axis):
        return getattr(self, axis)

    def step(self, axis, d):
        return self.dev(**{axis: (self.coord(axis) + d) % 4})

    def peer(self, dc, dxl, dy):
        c, xl, y = (self.c + dc) % 2, (self.xl + dxl) % 2, (self.y + dy) % 4
        return self.dev(x=self.xh * 2 + xl, y=y, c=c), c * 8 + xl * 4 + y

    def far(self, dz, dxh):
        return self.dev(z=(self.z + dz) % 4, x=(self.xh + dxh) % 2 * 2 + self.xl)


PEERS = tuple((dc, dxl, dy) for dc in range(2) for dxl in range(2) for dy in range(4) if (dc, dxl, dy) != (0, 0, 0))
FARS = tuple((dz, dxh) for dz in range(4) for dxh in range(2) if (dz, dxh) != (0, 0))


def blocks(rect):
    t, n, z, xh = rect
    nz, nxh = (4 if z is ALL else 1), (2 if xh is ALL else 1)

    def at(b):
        return (t + b // (nz * nxh), b // nxh % nz if z is ALL else z, b % nxh if xh is ALL else xh)

    return n * nz * nxh, at


def back_slots():
    slots = 0
    for w in BACK_WAVES:
        for color in w.colors():
            for _, rect in w.chain(color, Zero):
                slots += 3 * blocks(rect(0))[0]
    return slots


class Zero:
    z = xh = c = xl = y = x = s = 0


BACK_SLOTS = back_slots()
COPIES = sum((len(w.chain(k, Zero)) * 8 + 2) for w in OUT_WAVES + BACK_WAVES for k in w.colors()) + 3 * len(PEERS) + len(FARS) + 8


def view(ref, rect, half=None):
    t, n, z, xh = rect
    rows = ALL if half is None else pl.ds(48 * half, 48)
    return ref.at[pl.ds(t, n), z, xh, rows]


def f32(*shape):
    return pltpu.VMEM(shape, F32)


def b16(*shape):
    return pltpu.VMEM(shape, BF16)


INPUTS = ("norm_gain", "init_bias", "inner_gain", "inner_bias", "post_gain", "post_bias", "mlp_gain", "bias_rate", "tok", "cot",
          "wq", "wk", "wv", "wo", "wg", "wu", "wd", "init", "rate")
SCRATCH = dict(
    norm_gain=b16(1, 6), init_bias=b16(1, 6), inner_gain=b16(1, 6), inner_bias=b16(1, 6), post_gain=b16(1, 6), post_bias=b16(1, 6),
    mlp_gain=b16(1, 6), bias_rate=b16(1, HEADS), tok=b16(S, D), cot=b16(S, D), wq=b16(6, 768), wk=b16(6, 768), wv=b16(6, 768),
    wo=b16(6, 768), wg=b16(6, FF), wu=b16(6, FF), wd=b16(6, FF), init=b16(6, HEAD), rate=b16(6, HEADS), small=f32(6, 128),
    w4=b16(TILES, 4, 2, 96, 128), g4=b16(TILES, 4, 2, 96, 128), rc=b16(LAST.half + MID.half, 4, 2, 96, 128),
    land=b16(BACK_SLOTS, 96, 128), pk=b16(16, PROWS, 128), pkf=f32(16, PROWS, 128), rv=b16(16, PROWS, 128),
    rv2=b16(16, PROWS, 128), stf=f32(96, 128), sa=f32(16, 8, 128), sb=f32(8, 8, 128), stat=f32(8, 128), stat_sum=f32(8, 128),
    nrm=b16(S, D), q=f32(S, D), k=f32(S, D), v=f32(S, D), zc=f32(S, D), zq=f32(S, D), u=f32(S, D), gh=b16(S, D), gl=b16(S, D),
    s1=f32(S, D), c1=f32(S, D), e1=f32(S, D), y1=f32(S, D), n1=f32(S, D), n2=f32(S, D), s2=f32(S, D),
    mix=f32(S, D), hid=f32(S, D), post=b16(S, D), dzb=b16(S, D), dzc=b16(S, D), dgr=f32(S, D), dzf=f32(S, D),
    kbd=b16(GROUPS, 512, 256), qbd=b16(GROUPS, 512, 256), gbd=b16(GROUPS, 512, 256), dbd=b16(GROUPS, 512, 256),
    zbd=b16(GROUPS, 512, 256), pm=b16(GROUPS, S, 512), pmt=b16(GROUPS, S, 512), skk=f32(GROUPS, S, 512), sqk=f32(GROUPS, S, 512),
    rr=f32(GROUPS, S, 512), pscale=f32(S, 128), hcot=f32(S, D), bcot=b16(S, D), tcot=f32(S, D), ot=f32(S, D), out=b16(S, D),
    gtok=b16(S, D),
    nrm2=b16(2, S, D), mcot=b16(2, S, D), xt=b16(2, D, 2 * S), t2=f32(2, S, D), o2=f32(2, S, D), t_in=f32(S, D), o_in=f32(S, D),
    lsem=pltpu.SemaphoreType.DMA((len(INPUTS),)), ssem=pltpu.SemaphoreType.DMA((COPIES,)), rsem=pltpu.SemaphoreType.DMA((COPIES,)),
)


class Refs:
    def __init__(self, refs):
        for name, ref in zip(SCRATCH, refs, strict=True):
            setattr(self, name, ref)


def step_kernel(*refs):
    lens_ref = refs[0]
    hbm = refs[1 : 1 + len(INPUTS)]
    out_any, gtok_any, raw_any, stat_any = refs[1 + len(INPUTS) : 5 + len(INPUTS)]
    R = Refs(refs[5 + len(INPUTS) :])
    w4, g4, rc, land = R.w4, R.g4, R.rc, R.land
    me = Place()
    counter = [0]

    def send(src, dst, dev):
        i = counter[0]
        counter[0] += 1
        cp = pltpu.make_async_remote_copy(
            src_ref=src, dst_ref=dst, send_sem=R.ssem.at[i], recv_sem=R.rsem.at[i], device_id=dev, device_id_type=MESH
        )
        cp.start()
        return cp

    other = me.dev(c=1 - me.c)
    w3 = w4.reshape(TILES, D, 128)
    g3 = g4.reshape(TILES, D, 128)

    loads = {}
    for i, (name, src) in enumerate(zip(INPUTS, hbm)):
        cp = pltpu.make_async_copy(src, getattr(R, name), R.lsem.at[i])
        cp.start()
        loads[name] = cp

    barrier = pltpu.get_barrier_semaphore()
    greeted = 0
    for dev in [me.peer(*p)[0] for p in PEERS] + [me.step("x", d) for d in (1, 3)] + [me.far(*p) for p in FARS]:
        pl.semaphore_signal(barrier, inc=1, device_id=dev, device_id_type=MESH)
        greeted += 1
    for name, cp in loads.items():
        if name not in ("tok", "cot"):
            cp.wait()

    vec8 = jnp.concatenate([getattr(R, n)[...].astype(F32) for n in INPUTS[:7]] + [jnp.zeros((1, 6), F32)], axis=0).astype(BF16)
    R.small[...] = (
        nn(R.init[...], one_hot(iota((HEAD, 128), 0) == iota((HEAD, 128), 1)))
        + nn(R.rate[...], one_hot(iota((HEADS, 128), 0) + RATE0 == iota((HEADS, 128), 1)))
        + tn(vec8, one_hot(iota((8, 128), 0) + VEC0 == iota((8, 128), 1)))
    )
    bias_col = tt(one_hot(iota((HEADS, S), 0) + RATE0 == iota((HEADS, S), 1)), R.bias_rate[...])

    srcs = (R.wq, R.wk, R.wv, R.wo, R.wg, R.wu, R.wd, R.small)
    pkf, pk, rv, rv2, stf = R.pkf, R.pk, R.rv, R.rv2, R.stf
    pkf[0] = jnp.zeros((PROWS, 128), F32)
    for h in range(2):
        for xl in range(2):
            for y in range(4):
                i = 0
                for w in OUT_WAVES:
                    for n, t in enumerate(w.mine(h, xl, y)):
                        where = tile_source(w, h, t)
                        if where is not None and (y == 0 or n >= w.nx + w.nz):
                            a, col = where
                            pkf[0, pl.ds(6 * i, 6), :] = srcs[a][:, 128 * col : 128 * col + 128].astype(F32)
                        i += 1
                pk[h * 8 + xl * 4 + y] = pkf[0].astype(BF16)
    pl.semaphore_wait(barrier, greeted)
    firsts = []
    for p in PEERS:
        dev, slot = me.peer(*p)
        firsts.append(send(pk.at[slot], rv.at[me.s], dev))
    rv[pl.ds(me.s, 1)] = pk[pl.ds(me.s, 1)]

    ones = jnp.where(iota((256, 256), 0) // HEAD == iota((256, 256), 1) // HEAD, 1.0 / HEAD, 0.0).astype(BF16)
    rowtok = iota((S, 1), 0)
    mask_r, seg_r = layout_rows(lens_ref, rowtok)
    lane = iota((1, 512), 1)
    ltok = lane // 64 * 16 + lane % 16
    _, seg_l = layout_rows(lens_ref, ltok)
    loads["tok"].wait()
    loads["cot"].wait()
    R.mcot[pl.ds(me.c, 1)] = (R.cot[...].astype(F32) * mask_r).astype(BF16)[None]
    mc_copy = send(R.mcot.at[me.c], R.mcot.at[me.c], other)

    for cp in firsts:
        cp.wait_recv()
    for s in range(16):
        pkf[s] = rv[s].astype(F32)

    def unpack(w, i0):
        for i, t in enumerate(w.mine(me.c, me.xl, me.y)):
            for s in range(16):
                stf[pl.ds(6 * s, 6), :] = pkf[s, pl.ds(6 * (i0 + i), 6), :]
            w4[t, me.z, me.xh] = stf[...].astype(BF16)

    def gather(w, color, forward=()):
        sent = []
        for n, (axis, rect) in enumerate(w.chain(color, me)):
            at = me.coord(axis)
            mine, lo, hi = rect(at), rect((at + 3) % 4), rect((at + 1) % 4)
            now = [send(view(w4, mine), view(w4, mine), me.step(axis, d)) for d in ((1, 3) if n in forward else (1, 3, 2))]
            sent += now
            yield
            for cp in now:
                cp.wait_recv()
            if n in forward:
                now = [
                    send(view(w4, lo, 0), view(w4, lo, 0), me.step(axis, 1)),
                    send(view(w4, hi, 1), view(w4, hi, 1), me.step(axis, 3)),
                ]
                sent += now
                yield
                for cp in now:
                    cp.wait_recv()
        if not w.split:
            off, cnt = w.span(color)
            rect = (w.start(me.c) + off, cnt, ALL, ALL)
            a = send(view(w4, rect), view(w4, rect), other)
            sent.append(a)
            yield
            a.wait_recv()
        for cp in sent:
            cp.wait_send()

    def go(*chains):
        for ch in chains:
            next(ch, None)

    def finish(*chains):
        live = list(chains)
        while live:
            for ch in list(live):
                try:
                    next(ch)
                except StopIteration:
                    live.remove(ch)

    unpack(ONE, 0)
    one_x, one_z = gather(ONE, "x"), gather(ONE, "z")
    three_x = gather(THREE, "x")
    two_x, two_z, two_y = gather(TWO, "x", (1,)), gather(TWO, "z", (1,)), gather(TWO, "y", (2,))
    go(one_x, one_z)
    unpack(THREE, ONE.per)
    unpack(TWO, ONE.per + THREE.per)
    go(two_y, two_x, two_z, three_x)
    go(one_x, one_z)
    go(two_y)
    go(one_x, one_z)
    go(two_x, two_z, two_y, three_x)
    go(one_x, one_z)
    for cp in firsts:
        cp.wait_send()

    def wpair(t):
        return jnp.concatenate([w3[t], w3[t + 1]], axis=1)

    small = w3[TS]
    vsel = one_hot(iota((16, 128), 1) == iota((16, 128), 0) + VEC0)
    vecs = nt(vsel, small)
    norm_gain, init_bias, inner_gain, inner_bias, post_gain, post_bias, mlp_gain = (vecs[i : i + 1] for i in range(7))

    for i in range(4):
        rows = pl.ds(32 * i, 32)
        x = R.tok[rows, :].astype(F32)
        r = lax.rsqrt(jnp.mean(x * x, axis=-1, keepdims=True) + EPS)
        R.nrm[rows, :] = (x * r * norm_gain).astype(BF16)
    normed = R.nrm[...]
    for g in range(GROUPS):
        R.q[:, lanes(g)] = nn(normed, wpair(TQ + 2 * g))
        R.k[:, lanes(g)] = nn(normed, wpair(TK + 2 * g))
        R.v[:, lanes(g)] = nn(normed, wpair(TV + 2 * g))
    sig_t = jax.nn.sigmoid(tt(small, normed) + bias_col)
    rate_t = sig_t * (1.0 / HEAD)
    srow = iota((S, S), 0)
    is_rate = (srow >= RATE0) & (srow < RATE0 + HEADS)
    mask_tok, _ = layout_rows(lens_ref, iota((1, S), 1))
    live = jnp.where(is_rate, rate_t * mask_tok, 0.0)
    rate_sum = jnp.sum(live)
    rate_max = jnp.max(live)
    count = jnp.sum(mask_tok) * HEADS

    tsel = one_hot(iota((S, 512), 0) == ltok)
    rt_hi, rt_lo = split2(rate_t)
    rate_x = nn(rt_hi, tsel) + nn(rt_lo, tsel)
    lane_head = lane // 16 % 4
    jrow = iota((S, 512), 0)
    rate_lane = []
    for g in range(GROUPS):
        here = jrow == RATE0 + 4 * g + lane_head
        rate_lane.append(jnp.sum(jnp.where(here, rate_x, 0.0), axis=0, keepdims=True))
        sel = one_hot(here)
        R.rr[g] = tn(rt_hi, sel) + tn(rt_lo, sel)

    same = seg_r == seg_l
    rmb, rin = rowtok // 16, rowtok % 16
    lmb, lin = lane // 64, lane % 16

    def before():
        return jnp.where(same & (rmb > lmb), 1.0 / MINI, 0.0)

    def after():
        return jnp.where(same & (rmb < lmb), 1.0 / MINI, 0.0)

    def k2():
        return before() + jnp.where((rmb == lmb) & (lin <= rin), 1.0 / (rin + 1).astype(F32), 0.0)

    def k2t():
        return after() + jnp.where((rmb == lmb) & (rin <= lin), 1.0 / (lin + 1).astype(F32), 0.0)

    rep = one_hot(iota((S, 256), 0) == iota((S, 256), 1) % HEAD)
    b0c = init_bias - jnp.concatenate([nn(init_bias[:, 256 * g : 256 * g + 256].astype(BF16), ones) for g in range(GROUPS)], axis=1)
    diag = iota((256, 256), 0) // HEAD == iota((256, 256), 1) // HEAD
    gain2 = inner_gain * inner_gain

    def w0(g):
        wide = nn(w3[TS, 256 * g : 256 * g + 256, :], rep)
        wide = wide - jnp.mean(wide, axis=-1, keepdims=True)
        return split2(jnp.where(diag, wide, 0.0))

    R.u[...] = inner_gain * (inner_bias - R.v[...] + R.k[...])
    for g in range(GROUPS):
        gl = slice(256 * g, 256 * g + 256)
        kb, kl = split2(R.k[:, lanes(g)])
        qb, ql = split2(R.q[:, lanes(g)])
        for m in range(8):
            rows, here = pl.ds(64 * m, 64), slice(16 * m, 16 * m + 16)
            R.kbd[g, rows, :] = block_rows(kb[here])
            R.dbd[g, rows, :] = block_rows(kl[here])
            R.qbd[g, rows, :] = block_rows(qb[here])
        sc = nt(jnp.concatenate([kb, qb, ql], axis=0), R.kbd[g])
        sk = sc[:S] + 1.0
        R.skk[g] = sk
        R.sqk[g] = sc[S : 2 * S] + sc[2 * S :] + nt(qb, R.dbd[g]) + 1.0
        R.pm[g] = (sk * before() * rate_lane[g]).astype(BF16)
        R.pmt[g] = (sk * after() * R.rr[g]).astype(BF16)
        wh, wl = w0(g)
        zz = nn(jnp.concatenate([kb, qb, kl, ql], axis=0), wh)
        zl = nn(jnp.concatenate([kb, qb], axis=0), wl)
        R.zc[:, lanes(g)] = zz[:S] + zz[2 * S : 3 * S] + zl[:S] + b0c[:, gl]
        R.zq[:, lanes(g)] = zz[S : 2 * S] + zz[3 * S :] + zl[S:] + b0c[:, gl]

    def by_group(fn):
        return jnp.concatenate([fn(g, slice(256 * g, 256 * g + 256)) for g in range(GROUPS)], axis=1)

    def seg_mean(x):
        xb = x.astype(BF16)
        return by_group(lambda g, gl: nn(xb[:, gl], ones))

    def seg_mean2(x):
        n = x.shape[0]
        both = jnp.concatenate(split2(x), axis=0)
        r = by_group(lambda g, gl: nn(both[:, gl], ones))
        return r[:n] + r[n:]

    for m in range(8):
        rows = pl.ds(16 * m, 16)
        z = R.zc[rows, :]
        if m > 0:
            h = (m - 1) // 2 * 128
            if h > 0:
                z = z - by_group(lambda g, gl: nn(R.pm[g, rows, 0:h], R.gbd[g, 0:h, :]))
            z = z - by_group(lambda g, gl: nn(R.pm[g, rows, h : 64 * m], R.gbd[g, h : 64 * m, :]))
        uu = R.u[rows, :]
        gz = gain2 * z
        red = seg_mean2(jnp.concatenate([z * z, gz, gz * z, uu * z, uu], axis=0))
        var, r_gz, r_gzz, r_uz, r_u = (red[16 * i : 16 * i + 16] for i in range(5))
        s = lax.rsqrt(var + EPS)
        mg = s * r_gz
        mgg = s * s * r_gzz
        c = mgg + s * r_uz
        zh = z * s
        e = gain2 * zh + uu
        y = e - (mg + r_u) - zh * c
        gh, glow = split2(mask_r[16 * m : 16 * m + 16] * s * y)
        for g in range(GROUPS):
            R.gbd[g, pl.ds(64 * m, 64), :] = block_rows(gh[:, 256 * g : 256 * g + 256])
        R.gh[rows, :] = gh
        R.gl[rows, :] = glow
        R.zc[rows, :] = zh
        R.s1[rows, :] = s
        R.c1[rows, :] = c
        R.e1[rows, :] = e
        R.y1[rows, :] = y
        R.n1[rows, :] = mg
        R.n2[rows, :] = mgg
        if m == 3:
            go(two_x, two_z)
    for g in range(GROUPS):
        gl = slice(256 * g, 256 * g + 256)
        for m in range(8):
            R.dbd[g, pl.ds(64 * m, 64), :] = block_rows(R.gl[16 * m : 16 * m + 16, gl])
        ah, al = split2(R.sqk[g] * (k2() * rate_lane[g]))
        za = nn(jnp.concatenate([ah, al], axis=0), R.gbd[g])
        zb = R.zq[:, lanes(g)] - (za[:S] + za[S:] + nn(ah, R.dbd[g]))
        both = jnp.concatenate(split2(zb * zb), axis=0)
        var = nn(both, ones)
        s2 = lax.rsqrt(var[:S] + var[S:] + EPS)
        zh2 = zb * s2
        R.zq[:, lanes(g)] = zh2
        R.s2[:, lanes(g)] = s2
        R.mix[:, lanes(g)] = R.q[:, lanes(g)] + zh2 * inner_gain[:, gl] + inner_bias[:, gl]

    for i in range(4):
        rows = pl.ds(32 * i, 32)
        x = R.mix[rows, :]
        x = x - jnp.mean(x, axis=-1, keepdims=True)
        p_ = lax.rsqrt(jnp.mean(x * x, axis=-1, keepdims=True) + EPS)
        phat = x * p_
        R.mix[rows, :] = phat
        R.pscale[rows, :] = jnp.broadcast_to(p_, (32, 128))
        R.post[rows, :] = (phat * post_gain + post_bias).astype(BF16)
    pb = R.post[...]
    mc_copy.wait_recv()
    R.xt[1] = R.mcot[...].reshape(2 * S, D).T
    go(two_y)
    finish(three_x, one_x, one_z)

    def out_pair(g):
        return jnp.concatenate([w3[tile_out(2 * g)], w3[tile_out(2 * g + 1)]], axis=1)

    for g in range(GROUPS):
        R.hid[:, lanes(g)] = R.tok[:, lanes(g)].astype(F32) + nn(pb, out_pair(g))
    for i in range(4):
        rows = pl.ds(32 * i, 32)
        x = R.hid[rows, :]
        r = lax.rsqrt(jnp.mean(x * x, axis=-1, keepdims=True) + EPS)
        R.nrm2[pl.ds(me.c, 1), rows, :] = (x * r * mlp_gain).astype(BF16)[None]
    n2_copy = send(R.nrm2.at[me.c], R.nrm2.at[me.c], other)
    for t in PADS:
        g3[t] = jnp.zeros((D, 128), BF16)
    n2_copy.wait_recv()
    R.xt[0] = R.nrm2[...].reshape(2 * S, D).T
    finish(two_x, two_z, two_y)

    used = [0]

    def reduce(w, color, forward=()):
        off, cnt = w.span(color)
        sent = []
        if not w.split:
            landed = (0 if w is LAST else LAST.half) + off
            own = w.start(me.c) + off
            a = send(g4.at[pl.ds(w.start(1 - me.c) + off, cnt)], rc.at[pl.ds(landed, cnt)], other)
            sent.append(a)
            yield
            a.wait_recv()

            def add_tile(t, carry):
                for z in range(4):
                    for xh in range(2):
                        g4[own + t, z, xh] = (g4[own + t, z, xh].astype(F32) + rc[landed + t, z, xh].astype(F32)).astype(BF16)
                return carry

            lax.fori_loop(0, cnt, add_tile, 0)
        for n, (axis, rect) in enumerate(reversed(w.chain(color, me))):
            at = me.coord(axis)
            size, place = blocks(rect(at))
            base = used[0]
            used[0] += 3 * size
            _, nt_, z, xh = rect(at)
            lead = (nt_,) + ((4,) if z is ALL else ()) + ((2,) if xh is ALL else ())

            def slot(i, half=None, base=base, size=size, lead=lead):
                rows = ALL if half is None else pl.ds(48 * half, 48)
                return land.at[pl.ds(base + i * size, size)].reshape(*lead, 96, 128).at[(ALL,) * len(lead) + (rows,)]

            right, left, far = rect((at + 1) % 4), rect((at + 3) % 4), rect((at + 2) % 4)
            if n in forward:
                now = [
                    send(view(g4, far, 0), slot(2, 0), me.step(axis, 1)),
                    send(view(g4, far, 1), slot(2, 1), me.step(axis, 3)),
                ]
                sent += now
                yield
                for cp in now:
                    cp.wait_recv()
                right_at, left_at = blocks(right)[1], blocks(left)[1]

                def add_far(i, carry, base=base, size=size, right_at=right_at, left_at=left_at):
                    for half, where in ((0, right_at), (1, left_at)):
                        p = where(i) + (pl.ds(48 * half, 48),)
                        g4[p] = (g4[p].astype(F32) + land[base + 2 * size + i, pl.ds(48 * half, 48)].astype(F32)).astype(BF16)
                    return carry

                lax.fori_loop(0, size, add_far, 0)
                now = [send(view(g4, right), slot(0), me.step(axis, 1)), send(view(g4, left), slot(1), me.step(axis, 3))]
            else:
                now = [
                    send(view(g4, right), slot(0), me.step(axis, 1)),
                    send(view(g4, left), slot(1), me.step(axis, 3)),
                    send(view(g4, far), slot(2), me.step(axis, 2)),
                ]
            sent += now
            yield
            for cp in now:
                cp.wait_recv()
            terms = len(now)

            def add_mine(i, carry, base=base, size=size, place=place, terms=terms):
                p = place(i)
                total = g4[p].astype(F32)
                for k_ in range(terms):
                    total += land[base + k_ * size + i].astype(F32)
                g4[p] = total.astype(BF16)
                return carry

            lax.fori_loop(0, size, add_mine, 0)
        for cp in sent:
            cp.wait_send()

    back_y, back_z, back_x = reduce(FIRST, "y", (0,)), reduce(FIRST, "z", (0,)), reduce(FIRST, "x", (0,))

    x2, mc = R.nrm2[...].reshape(2 * S, D), R.mcot[...].reshape(2 * S, D)
    for j in reversed(range(4)):
        wg, wu, wd = (wpair(tile_mlp(j, kind)) for kind in range(3))
        gate, up, ac = nn(x2, wg), nn(x2, wu), nn(mc, wd)
        sg = jax.nn.sigmoid(gate)
        silu = gate * sg
        a = (silu * up).astype(BF16)
        gc = (ac * up * (sg * (1.0 + gate * (1.0 - sg)))).astype(BF16)
        uc = (ac * silu).astype(BF16)
        o_part = nt(a, wd).reshape(2, S, D)
        t_part = (nt(gc, wg) + nt(uc, wu)).reshape(2, S, D)
        if j == 3:
            R.o2[...] = o_part
            R.t2[...] = t_part
        else:
            R.o2[...] += o_part
            R.t2[...] += t_part
        for h in range(2):
            sl = slice(128 * h, 128 * h + 128)
            g3[tile_mlp(j, 0) + h] = nn(R.xt[0], gc[:, sl]).astype(BF16)
            g3[tile_mlp(j, 1) + h] = nn(R.xt[0], uc[:, sl]).astype(BF16)
            g3[tile_mlp(j, 2) + h] = nn(R.xt[1], a[:, sl]).astype(BF16)
        if j == 2:
            go(back_y)
        if j == 1:
            go(back_z)
    t_copy = send(R.t2.at[1 - me.c], R.t_in, other)
    go(back_x)
    o_copy = send(R.o2.at[1 - me.c], R.o_in, other)

    t_copy.wait_recv()
    g_mlp_gain = jnp.zeros((1, D), F32)
    for i in range(4):
        rows = pl.ds(32 * i, 32)
        mr = mask_r[32 * i : 32 * i + 32]
        x = R.hid[rows, :]
        r = lax.rsqrt(jnp.mean(x * x, axis=-1, keepdims=True) + EPS)
        u = x * r
        t = R.t2[pl.ds(me.c, 1), rows, :][0] + R.t_in[rows, :]
        g_mlp_gain += jnp.sum(t * u, axis=0, keepdims=True)
        c = t * mlp_gain
        h = mr * R.cot[rows, :].astype(F32) + r * (c - u * jnp.mean(c * u, axis=-1, keepdims=True))
        R.hcot[rows, :] = h
        R.bcot[rows, :] = h.astype(BF16)

    bc = R.bcot[...]
    pt_ = pb.T
    for c_ in range(6):
        g3[tile_out(c_)] = nn(pt_, bc[:, 128 * c_ : 128 * c_ + 128]).astype(BF16)
    go(back_y, back_z)
    acc = nt(bc[:, 0:256], out_pair(0))
    for g in range(1, GROUPS):
        acc += nt(bc[:, 256 * g : 256 * g + 256], out_pair(g))
    R.tcot[...] = acc
    go(back_x)
    o_copy.wait_recv()
    for i in range(4):
        rows = pl.ds(32 * i, 32)
        o = R.hid[rows, :] + R.o2[pl.ds(me.c, 1), rows, :][0] + R.o_in[rows, :]
        R.out[rows, :] = (mask_r[32 * i : 32 * i + 32] * o).astype(BF16)
    out_copy = pltpu.make_async_copy(R.out, out_any, R.lsem.at[0])
    out_copy.start()
    g_post_gain = jnp.zeros((1, D), F32)
    g_post_bias = jnp.zeros((1, D), F32)
    for i in range(4):
        rows = pl.ds(32 * i, 32)
        pc = R.tcot[rows, :]
        phat = R.mix[rows, :]
        g_post_gain += jnp.sum(pc * phat, axis=0, keepdims=True)
        g_post_bias += jnp.sum(pc, axis=0, keepdims=True)
        e = pc * post_gain
        R.tcot[rows, :] = R.pscale[rows, 0:1] * (
            e - jnp.mean(e, axis=-1, keepdims=True) - phat * jnp.mean(e * phat, axis=-1, keepdims=True)
        )

    do, zh2 = R.tcot[...], R.zq[...]
    g_inner_gain = jnp.sum(do * zh2, axis=0, keepdims=True)
    g_inner_bias = jnp.sum(do, axis=0, keepdims=True)
    dz = do * inner_gain
    dzb = R.s2[...] * (dz - zh2 * seg_mean(dz * zh2))
    gb_rows = jnp.sum(dzb, axis=0, keepdims=True)
    R.dzb[...] = dzb.astype(BF16)
    R.zbd[...] = jnp.zeros(R.zbd.shape, BF16)
    for g in range(GROUPS):
        db = R.dzb[:, lanes(g)]
        for m in range(8):
            R.dbd[g, pl.ds(64 * m, 64), :] = block_rows(db[16 * m : 16 * m + 16])
        kb = R.k[:, lanes(g)].astype(BF16)
        at = (nt(kb, R.qbd[g]) + 1.0) * (k2t() * R.rr[g])
        R.dgr[:, lanes(g)] = -nn(at.astype(BF16), R.dbd[g])

    for m in reversed(range(8)):
        rows = pl.ds(16 * m, 16)
        dg = R.dgr[rows, :]
        if m < 7:
            h = (m + 1) // 2 * 128
            if h + 128 < 512:
                dg = dg - by_group(lambda g, gl: nn(R.pmt[g, rows, h + 128 : 512], R.zbd[g, h + 128 : 512, :]))
            dg = dg - by_group(lambda g, gl: nn(R.pmt[g, rows, h : h + 128], R.zbd[g, h : h + 128, :]))
        hh = mask_r[16 * m : 16 * m + 16] * dg
        s, c, zh, e, y = R.s1[rows, :], R.c1[rows, :], R.zc[rows, :], R.e1[rows, :], R.y1[rows, :]
        zhh = zh * hh
        red = seg_mean(jnp.concatenate([hh, zhh, gain2 * zhh, y * hh], axis=0))
        m0, m1, m2, m3 = (red[16 * i : 16 * i + 16] for i in range(4))
        de = s * (hh - m0 - zh * m1)
        dzh = gain2 * de - s * (c * hh + e * m1)
        t = m2 - 2.0 * c * m1 - m0 * R.n1[rows, :] - m1 * R.n2[rows, :]
        dzc = s * (dzh - zh * (s * (m3 + t)))
        db = dzc.astype(BF16)
        for g in range(GROUPS):
            R.zbd[g, pl.ds(64 * m, 64), :] = block_rows(db[:, 256 * g : 256 * g + 256])
        R.dzc[rows, :] = db
        R.dgr[rows, :] = de
        R.dzf[rows, :] = dzc

    de = R.dgr[...]
    g_inner_gain += jnp.sum(de * (inner_bias - R.v[...] + R.k[...] + 2.0 * inner_gain * R.zc[...]), axis=0, keepdims=True)
    gde_all = inner_gain * de
    g_inner_bias += jnp.sum(gde_all, axis=0, keepdims=True)
    bsum = gb_rows + jnp.sum(R.dzf[...], axis=0, keepdims=True)
    g_init_bias = bsum - seg_mean2(jnp.broadcast_to(bsum, (16, D)))[0:1]
    x1t = R.nrm[...].T
    dv_all = (-gde_all).astype(BF16)
    for c_ in range(6):
        g3[TV + c_] = nn(x1t, dv_all[:, 128 * c_ : 128 * c_ + 128]).astype(BF16)
    mid_x, mid_z = reduce(MID, "x"), reduce(MID, "z")
    go(mid_x, mid_z)
    logit_acc = jnp.zeros((S, S), F32)
    wgrad_small = []
    for g in range(GROUPS):
        gl = slice(256 * g, 256 * g + 256)
        gde = inner_gain[:, gl] * R.dgr[:, lanes(g)]
        dzb_b, dzc_b = R.dzb[:, lanes(g)], R.dzc[:, lanes(g)]
        kb = R.k[:, lanes(g)].astype(BF16)
        qb = R.q[:, lanes(g)].astype(BF16)
        gb = R.gh[:, lanes(g)]
        rl, rr = rate_lane[g], R.rr[g]
        dd = nt(jnp.concatenate([dzb_b, dzc_b], axis=0), R.gbd[g])
        dr = -dd[:S] * k2()
        dp = -dd[S:] * before()
        drate = jnp.sum(dr * R.sqk[g] + dp * R.skk[g], axis=0, keepdims=True)
        dat = -nt(gb, R.dbd[g])
        dpt = -nt(gb, R.zbd[g])
        low = jnp.concatenate([(dr * rl).astype(BF16), (dp * rl + dpt * (after() * rr)).astype(BF16)], axis=0)
        dqk = nn(low, R.kbd[g])
        wh, _ = w0(g)
        dqk += nt(jnp.concatenate([dzb_b, dzc_b], axis=0), wh)
        dq = R.tcot[:, lanes(g)] + dqk[:S]
        dk = gde + dqk[S:] + nn((dat * (k2t() * rr)).astype(BF16), R.qbd[g])
        gwide = jnp.where(diag, tn(qb, dzb_b) + tn(kb, dzc_b), 0.0)
        fold = one_hot(iota((256, 128), 0) % HEAD == iota((256, 128), 1))
        gw_hi, gw_lo = split2(gwide)
        gsm = nn(gw_hi, fold) + nn(gw_lo, fold)
        wgrad_small.append(
            gsm - jnp.where(iota((256, 128), 1) < HEAD, jnp.sum(gsm, axis=-1, keepdims=True) * (1.0 / HEAD), 0.0)
        )
        dl = drate * rl * (1.0 - rl * HEAD)
        dlx = jnp.where(jrow == RATE0 + 4 * g + lane_head, dl, 0.0)
        logit_acc += nt(dlx.astype(BF16), tsel)
        dqb, dkb, dvb = dq.astype(BF16), dk.astype(BF16), (-gde).astype(BF16)
        for h in range(2):
            sl = slice(128 * h, 128 * h + 128)
            g3[TQ + 2 * g + h] = nn(x1t, dqb[:, sl]).astype(BF16)
            g3[TK + 2 * g + h] = nn(x1t, dkb[:, sl]).astype(BF16)
        part = nt(dqb, wpair(TQ + 2 * g)) + nt(dkb, wpair(TK + 2 * g)) + nt(dvb, wpair(TV + 2 * g))
        if g == 0:
            R.ot[...] = part
        else:
            R.ot[...] += part

    last_x, last_z = reduce(LAST, "x"), reduce(LAST, "z")
    go(last_x, mid_x, mid_z, back_y)
    logit_b = logit_acc.astype(BF16)
    oc_all = R.ot[...] + tt(logit_b, small)
    R.ot[...] = oc_all
    g_bias = jnp.sum(logit_acc, axis=1, keepdims=True)
    g_rate = nt(x1t, logit_b)
    g_norm_gain = jnp.zeros((1, D), F32)
    for i in range(4):
        rows = pl.ds(32 * i, 32)
        x = R.tok[rows, :].astype(F32)
        r = lax.rsqrt(jnp.mean(x * x, axis=-1, keepdims=True) + EPS)
        g_norm_gain += jnp.sum(R.ot[rows, :] * (x * r), axis=0, keepdims=True)

    vec_rows = jnp.concatenate(
        [g_norm_gain, g_init_bias, g_inner_gain, g_inner_bias, g_post_gain, g_post_bias, g_mlp_gain, jnp.zeros((9, D), F32)], axis=0
    ).astype(BF16)
    g3[TS] = (jnp.concatenate(wgrad_small, axis=0) + g_rate + tn(vec_rows, vsel)).astype(BF16)
    go(last_z)

    bias_row = jnp.sum(jnp.where(iota((S, S), 0) == iota((S, S), 1), g_bias, 0.0), axis=0, keepdims=True)
    r8 = iota((8, 128), 0)
    R.stat[...] = jnp.where(
        r8 == 0, rate_sum, jnp.where(r8 == 1, count, jnp.where(r8 == 2, rate_max, jnp.where(r8 == 3, bias_row, 0.0)))
    )
    stats = [send(R.stat, R.sa.at[me.s], me.peer(*p)[0]) for p in PEERS]
    R.sa[pl.ds(me.s, 1)] = R.stat[...][None]
    for i in range(4):
        rows = pl.ds(32 * i, 32)
        x = R.tok[rows, :].astype(F32)
        r = lax.rsqrt(jnp.mean(x * x, axis=-1, keepdims=True) + EPS)
        w = x * r
        f = R.ot[rows, :] * norm_gain
        R.gtok[rows, :] = (R.hcot[rows, :] + r * (f - w * jnp.mean(f * w, axis=-1, keepdims=True))).astype(BF16)
    gtok_copy = pltpu.make_async_copy(R.gtok, gtok_any, R.lsem.at[1])
    gtok_copy.start()

    go(last_x, back_z, back_x, last_z)

    def combine(buf, n):
        total, peak = buf[0], buf[0]
        for s in range(1, n):
            total, peak = total + buf[s], jnp.maximum(peak, buf[s])
        return jnp.where(r8 == 2, peak, total)

    for cp in stats:
        cp.wait_recv()
    R.sb[pl.ds(me.zx, 1)] = combine(R.sa, 16)[None]
    stats2 = [send(R.sb.at[me.zx], R.sb.at[me.zx], me.far(*p)) for p in FARS]
    finish(mid_x, mid_z, back_y, last_x, last_z, back_z, back_x)

    i = 0
    for w in BACK_WAVES:
        for t in w.mine(me.c, me.xl, me.y):
            stf[...] = g4[t, me.z, me.xh].astype(F32)
            for s in range(16):
                pkf[s, pl.ds(6 * i, 6), :] = stf[pl.ds(6 * s, 6), :]
            i += 1
    for s in range(16):
        pk[s] = pkf[s].astype(BF16)
    last = []
    for p in PEERS:
        dev, slot = me.peer(*p)
        last.append(send(pk.at[slot], rv2.at[me.s], dev))
    rv2[pl.ds(me.s, 1)] = pk[pl.ds(me.s, 1)]
    for cp in stats2:
        cp.wait_recv()
    R.stat_sum[...] = combine(R.sb, 8)
    stat_copy = pltpu.make_async_copy(R.stat_sum, stat_any, R.lsem.at[2])
    stat_copy.start()
    for cp in last:
        cp.wait_recv()
    raw_copy = pltpu.make_async_copy(rv2, raw_any, R.lsem.at[3])
    raw_copy.start()
    for cp in [mc_copy, n2_copy, t_copy, o_copy] + stats + stats2 + last:
        cp.wait_send()
    for cp in (out_copy, gtok_copy, stat_copy, raw_copy):
        cp.wait()


def step(lens, *arrays):
    anym = pl.BlockSpec(memory_space=pl.ANY)
    sd = jax.ShapeDtypeStruct
    return pl.pallas_call(
        step_kernel,
        out_shape=(sd((S, D), BF16), sd((S, D), BF16), sd((16, PROWS, 128), BF16), sd((8, 128), F32)),
        in_specs=[pl.BlockSpec(memory_space=pltpu.SMEM)] + [anym] * len(INPUTS),
        out_specs=(anym,) * 4,
        scratch_shapes=list(SCRATCH.values()),
        compiler_params=pltpu.CompilerParams(collective_id=0, has_side_effects=True, vmem_limit_bytes=60 * 2**20),
        name="step",
    )(lens, *arrays)


def finish_kernel(raw, stat, out_in, gtok_in, *outs):
    (out, gtok, g_norm, gq, gk, gv, g_rate, g_brate, g_init, g_ib, g_ig, g_ibias, g_pg, g_pb, go, g_mg, gg, gu, gd,
     r_mean, r_max, pkf) = outs
    out[...] = out_in[...]
    gtok[...] = gtok_in[...]
    mats = (gq, gk, gv, go, gg, gu, gd)
    for s in range(16):
        pkf[s] = raw[s].astype(F32)
    for h in range(2):
        for xl in range(2):
            i = 0
            for w in BACK_WAVES:
                for n in range(w.per):
                    for y in range(4 if n >= w.nx + w.nz else 1):
                        where = tile_source(w, h, w.mine(h, xl, y)[n])
                        if where is None:
                            continue
                        if n < w.nx + w.nz:
                            x = [pkf[h * 8 + xl * 4 + y_, pl.ds(6 * i, 6), :] for y_ in range(4)]
                            val = (x[0] + x[1]) + (x[2] + x[3])
                        else:
                            val = pkf[h * 8 + xl * 4 + y, pl.ds(6 * i, 6), :]
                        a, col = where
                        if a < A_S:
                            mats[a][:, 128 * col : 128 * col + 128] = val
                        else:
                            g_init[...] = val[:, :HEAD]
                            g_rate[...] = val[:, RATE0 : RATE0 + HEADS]
                            vt = val.T
                            for n_, ref in enumerate((g_norm, g_ib, g_ig, g_ibias, g_pg, g_pb, g_mg)):
                                ref[...] = vt[VEC0 + n_ : VEC0 + n_ + 1, :]
                    i += 1
    st = stat[...]
    g_brate[...] = st[3:4, RATE0 : RATE0 + HEADS]
    r_mean[...] = st[0:1, 0:1] / st[1:2, 0:1]
    r_max[...] = st[2:3, 0:1]


def finish_call(raw, stat, out, gtok):
    vm = pl.BlockSpec(memory_space=pltpu.VMEM)
    sd = jax.ShapeDtypeStruct
    row = sd((1, 6), F32)
    m768, m2048 = sd((6, 768), F32), sd((6, FF), F32)
    shapes = (
        sd((S, D), BF16), sd((S, D), BF16), row, m768, m768, m768, sd((6, HEADS), F32), sd((1, HEADS), F32),
        sd((6, HEAD), F32), row, row, row, row, row, m768, row, m2048, m2048, m2048, sd((1, 1), F32), sd((1, 1), F32),
    )
    return pl.pallas_call(
        finish_kernel, out_shape=shapes, in_specs=[vm] * 4, out_specs=(vm,) * 21,
        scratch_shapes=[pltpu.VMEM((16, PROWS, 128), F32)], name="finish",
    )(raw, stat, out, gtok)


def per_device(
    tokens, cotangent, seq_lengths, norm_gain, weight_query, weight_key, weight_value, weight_rate, bias_rate,
    init_weight, init_bias, inner_gain, inner_bias, post_gain, post_bias, weight_out, mlp_gain, weight_gate, weight_up,
    weight_down,
):
    rows = (norm_gain, init_bias, inner_gain, inner_bias, post_gain, post_bias, mlp_gain)
    out, gtok, raw, stat = step(
        seq_lengths, *[r.reshape(1, -1) for r in rows + (bias_rate,)], tokens, cotangent, weight_query, weight_key, weight_value, weight_out, weight_gate, weight_up,
        weight_down, init_weight, weight_rate,
    )
    res = list(finish_call(raw, stat, out, gtok))
    for i in (2, 9, 10, 11, 12, 13, 15):
        res[i] = res[i].reshape(6)
    res[7] = res[7].reshape(HEADS)
    res[19], res[20] = res[19].reshape(()), res[20].reshape(())
    return tuple(res)


def solution(mesh):
    both = ("dp", "sub")
    mat, vec, rep = P(both, None), P(both), P()
    return jax.shard_map(
        per_device,
        mesh=mesh,
        in_specs=(mat, mat, mat, vec, mat, mat, mat, mat, rep, mat, vec, vec, vec, vec, vec, mat, vec, mat, mat, mat),
        out_specs=(mat, mat, vec, mat, mat, mat, mat, rep, mat, vec, vec, vec, vec, vec, mat, vec, mat, mat, mat, rep, rep),
        check_vma=False,
    )
```

```python
import jax
import jax.numpy as jnp
from jax import lax
from jax.experimental import pallas as pl
from jax.experimental.pallas import tpu as pltpu
from jax.sharding import PartitionSpec as P

MESH = pl.DeviceIdType.MESH
HEADS = 12
HEAD = 64
MINI = 16
EPS = 1e-06
F32 = jnp.float32
BF16 = jnp.bfloat16
S = 128
D = 768
FF = 2048
GROUPS = 3
RATE0 = 64
VEC0 = 76
ALL = slice(None)


class Wave:
    def __init__(self, base, nx, nz, ny, split=False):
        self.base, self.nx, self.nz, self.ny = base, nx, nz, ny
        self.half = 2 * nx + 2 * nz + 8 * ny
        self.per = nx + nz + ny
        self.split = split

    def start(self, h):
        return self.base if self.split else self.base + h * self.half

    def tx(self, h, xl):
        return self.start(h) + xl * self.nx

    def tz(self, h, xl):
        return self.start(h) + 2 * self.nx + xl * self.nz

    def ty(self, h, y, xl):
        return self.start(h) + 2 * self.nx + 2 * self.nz + (y * 2 + xl) * self.ny

    def mine(self, h, xl, y):
        return (
            [self.tx(h, xl) + n for n in range(self.nx)]
            + [self.tz(h, xl) + n for n in range(self.nz)]
            + [self.ty(h, y, xl) + n for n in range(self.ny)]
        )

    def span(self, color):
        return {
            "x": (0, 2 * self.nx),
            "z": (2 * self.nx, 2 * self.nz),
            "y": (2 * self.nx + 2 * self.nz, 8 * self.ny),
        }[color]

    def chain(self, color, me):
        if color == "x":
            return [
                ("z", lambda p: (self.tx(me.c, me.xl), self.nx, p, me.xh)),
                ("x", lambda p: (self.tx(me.c, p % 2), self.nx, ALL, p // 2)),
            ]
        if color == "z":
            return [
                ("x", lambda p: (self.tz(me.c, p % 2), self.nz, me.z, p // 2)),
                ("z", lambda p: (self.tz(me.c, 0), 2 * self.nz, p, ALL)),
            ]
        return [
            ("z", lambda p: (self.ty(me.c, me.y, me.xl), self.ny, p, me.xh)),
            ("x", lambda p: (self.ty(me.c, me.y, p % 2), self.ny, ALL, p // 2)),
            ("y", lambda p: (self.ty(me.c, p, 0), 2 * self.ny, ALL, ALL)),
        ]

    def colors(self, order="xzy"):
        return [k for k in order if {"x": self.nx, "z": self.nz, "y": self.ny}[k]]


ONE, THREE, TWO = Wave(0, 3, 3, 0), Wave(24, 0, 1, 0), Wave(28, 4, 4, 1, split=True)
OUT_WAVES = (ONE, THREE, TWO)
LAST, MID, FIRST = Wave(0, 2, 2, 0), Wave(16, 1, 2, 0), Wave(28, 4, 4, 1, split=True)
BACK_WAVES = (LAST, MID, FIRST)
TILES = 52
PER = max(sum(w.per for w in ws) for ws in (OUT_WAVES, BACK_WAVES))
PROWS = (PER * 6 + 15) // 16 * 16
TQ, TK, TS, TV = 0, 6, 12, 16
PADS = (25, 26, 27)
A_Q, A_K, A_V, A_O, A_G, A_U, A_D, A_S = range(8)
WIDTHS = (768, 768, 768, 768, 2048, 2048, 2048, 128)


def tile_out(c):
    return 13 + c if c < 3 else 19 + c


def tile_mlp(j, kind):
    return TWO.base + 6 * j + 2 * kind


def tile_source(w, h, t):
    if w.split:
        o = t - w.base
        return A_G + o % 6 // 2, 8 * h + o // 6 * 2 + o % 2
    if t in PADS:
        return None
    for a, first in ((A_Q, TQ), (A_K, TK), (A_V, TV)):
        if first <= t < first + 6:
            return a, t - first
    if t == TS:
        return A_S, 0
    return A_O, t - 13 if t < TV else t - 19


def nn(a, b):
    return lax.dot_general(a, b, (((1,), (0,)), ((), ())), preferred_element_type=F32)


def nt(a, b):
    return lax.dot_general(a, b, (((1,), (1,)), ((), ())), preferred_element_type=F32)


def tn(a, b):
    return lax.dot_general(a, b, (((0,), (0,)), ((), ())), preferred_element_type=F32)


def tt(a, b):
    return lax.dot_general(a, b, (((0,), (1,)), ((), ())), preferred_element_type=F32)


def iota(shape, dim):
    return lax.broadcasted_iota(jnp.int32, shape, dim)


def one_hot(cond):
    return jnp.where(cond, 1.0, 0.0).astype(BF16)


def split2(x):
    hi = x.astype(BF16)
    return hi, (x - hi.astype(F32)).astype(BF16)


def head_select(x, h):
    return jnp.where(iota(x.shape, 1) // HEAD == h, x, jnp.zeros_like(x))


def block_rows(x):
    return jnp.concatenate([head_select(x, h) for h in range(4)], axis=0)


def lanes(g):
    return pl.ds(256 * g, 256)


def layout_rows(lens_ref, token):
    mask = jnp.zeros(token.shape, F32)
    seg = jnp.zeros(token.shape, F32)
    start = jnp.int32(0)
    for j in range(4):
        n = lens_ref[0, j]
        mask += jnp.where((token >= start) & (token < start + n), 1.0, 0.0)
        seg += jnp.where((token >= start) & (n > 0), 1.0, 0.0)
        start += (n + 15) // 16 * 16
    return mask, seg


class Place:
    def __init__(self):
        dp, sub = lax.axis_index("dp"), lax.axis_index("sub")
        self.z = dp // 4
        self.xh = dp // 2 % 2
        self.c = dp % 2
        self.xl = sub // 4
        self.y = sub % 4
        self.x = self.xh * 2 + self.xl
        self.s = self.c * 8 + sub
        self.zx = self.z * 2 + self.xh

    def dev(self, z=None, x=None, y=None, c=None):
        z = self.z if z is None else z
        x = self.x if x is None else x
        y = self.y if y is None else y
        c = self.c if c is None else c
        return (z * 4 + x // 2 * 2 + c, x % 2 * 4 + y)

    def coord(self, axis):
        return getattr(self, axis)

    def step(self, axis, d):
        return self.dev(**{axis: (self.coord(axis) + d) % 4})

    def peer(self, dc, dxl, dy):
        c, xl, y = (self.c + dc) % 2, (self.xl + dxl) % 2, (self.y + dy) % 4
        return self.dev(x=self.xh * 2 + xl, y=y, c=c), c * 8 + xl * 4 + y

    def far(self, dz, dxh):
        return self.dev(z=(self.z + dz) % 4, x=(self.xh + dxh) % 2 * 2 + self.xl)


PEERS = tuple((dc, dxl, dy) for dc in range(2) for dxl in range(2) for dy in range(4) if (dc, dxl, dy) != (0, 0, 0))
FARS = tuple((dz, dxh) for dz in range(4) for dxh in range(2) if (dz, dxh) != (0, 0))


def blocks(rect):
    t, n, z, xh = rect
    nz, nxh = (4 if z is ALL else 1), (2 if xh is ALL else 1)

    def at(b):
        return (t + b // (nz * nxh), b // nxh % nz if z is ALL else z, b % nxh if xh is ALL else xh)

    return n * nz * nxh, at


def back_slots():
    slots = 0
    for w in BACK_WAVES:
        for color in w.colors():
            for _, rect in w.chain(color, Zero):
                slots += 3 * blocks(rect(0))[0]
    return slots


class Zero:
    z = xh = c = xl = y = x = s = 0


BACK_SLOTS = back_slots()


def steps_forward(w, color, back):
    if w.split:
        if back:
            return {"x": (0,), "z": (0,), "y": (0, 1)}[color]
        return {"x": (1,), "z": (1,), "y": (1, 2)}[color]
    if back:
        return (0,)
    return (1,) if w is ONE else ()


def copies_of(w, color, back):
    fwd = steps_forward(w, color, back)
    return sum(4 if n in fwd else 3 for n in range(len(w.chain(color, Zero)))) + (0 if w.split else 1)


OUT_COPIES = sum(copies_of(w, k, False) for w in OUT_WAVES for k in w.colors())
BACK_COPIES = sum(copies_of(w, k, True) for w in BACK_WAVES for k in w.colors())
RECV_SEMS = OUT_COPIES + BACK_COPIES + 8
SEND_SEMS = max(OUT_COPIES, BACK_COPIES) + 8


def view(ref, rect, half=None):
    t, n, z, xh = rect
    rows = ALL if half is None else pl.ds(48 * half, 48)
    return ref.at[pl.ds(t, n), z, xh, rows]


def f32(*shape):
    return pltpu.VMEM(shape, F32)


def b16(*shape):
    return pltpu.VMEM(shape, BF16)


INPUTS = ("norm_gain", "init_bias", "inner_gain", "inner_bias", "post_gain", "post_bias", "mlp_gain", "bias_rate", "tok", "cot",
          "wq", "wk", "wv", "wo", "wg", "wu", "wd", "init", "rate")
SCRATCH = dict(
    norm_gain=b16(1, 6), init_bias=b16(1, 6), inner_gain=b16(1, 6), inner_bias=b16(1, 6), post_gain=b16(1, 6), post_bias=b16(1, 6),
    mlp_gain=b16(1, 6), bias_rate=b16(1, HEADS), tok=b16(S, D), cot=b16(S, D), wq=b16(6, 768), wk=b16(6, 768), wv=b16(6, 768),
    wo=b16(6, 768), wg=b16(6, FF), wu=b16(6, FF), wd=b16(6, FF), init=b16(6, HEAD), rate=b16(6, HEADS), small=f32(6, 128),
    w4=b16(TILES, 4, 2, 96, 128), g4=b16(TILES, 4, 2, 96, 128), rc=b16(LAST.half + MID.half, 4, 2, 96, 128),
    land=b16(BACK_SLOTS, 96, 128), pk=b16(16, PROWS, 128), pkf=f32(16, PROWS, 128), rv=b16(16, PROWS, 128),
    rv2=b16(16, PROWS, 128), stf=f32(96, 128), sa=f32(16, 8, 128), sb=f32(8, 8, 128), stat=f32(8, 128), stat_sum=f32(8, 128),
    nrm=b16(S, D), q=f32(S, D), k=f32(S, D), v=f32(S, D), zc=f32(S, D), zq=f32(S, D), u=f32(S, D), gh=b16(S, D), gl=b16(S, D),
    s1=f32(S, D), c1=f32(S, D), e1=f32(S, D), y1=f32(S, D), n1=f32(S, D), n2=f32(S, D), s2=f32(S, D),
    mix=f32(S, D), hid=f32(S, D), post=b16(S, D), dzb=b16(S, D), dzc=b16(S, D), dgr=f32(S, D), dzf=f32(S, D),
    kbd=b16(GROUPS, 512, 256), qbd=b16(GROUPS, 512, 256), gbd=b16(GROUPS, 512, 256), dbd=b16(GROUPS, 512, 256),
    zbd=b16(GROUPS, 512, 256), pm=b16(GROUPS, S, 512), pmt=b16(GROUPS, S, 512), skk=f32(GROUPS, S, 512), sqk=f32(GROUPS, S, 512),
    rr=f32(GROUPS, S, 512), pscale=f32(S, 128), hcot=f32(S, D), bcot=b16(S, D), tcot=f32(S, D), ot=f32(S, D), out=b16(S, D),
    gtok=b16(S, D),
    nrm2=b16(2, S, D), mcot=b16(2, S, D), xt=b16(2, D, 2 * S), t2=f32(2, S, D), o2=f32(2, S, D), t_in=f32(S, D), o_in=f32(S, D),
    lsem=pltpu.SemaphoreType.DMA((len(INPUTS),)), ssem=pltpu.SemaphoreType.DMA((SEND_SEMS,)), rsem=pltpu.SemaphoreType.DMA((RECV_SEMS,)),
)


class Refs:
    def __init__(self, refs):
        for name, ref in zip(SCRATCH, refs, strict=True):
            setattr(self, name, ref)


def step_kernel(*refs):
    lens_ref = refs[0]
    hbm = refs[1 : 1 + len(INPUTS)]
    out_any, gtok_any, raw_any, stat_any = refs[1 + len(INPUTS) : 5 + len(INPUTS)]
    R = Refs(refs[5 + len(INPUTS) :])
    w4, g4, rc, land = R.w4, R.g4, R.rc, R.land
    me = Place()
    taken = {"group": 0, "out": 8, "back": 8}

    def copy(src, dst, dev, i, j):
        return pltpu.make_async_remote_copy(
            src_ref=src, dst_ref=dst, send_sem=R.ssem.at[i], recv_sem=R.rsem.at[j], device_id=dev, device_id_type=MESH
        )

    def send(src, dst, dev, kind="group"):
        i = taken[kind]
        taken[kind] += 1
        cp = copy(src, dst, dev, i, i + OUT_COPIES if kind == "back" else i)
        cp.start()
        return cp

    def send_all(triples, whole):
        i = taken["group"]
        taken["group"] += 1
        for src, dst, dev in triples:
            copy(src, dst, dev, i, i).start()
        return copy(whole, whole, me.dev(), i, i)

    other = me.dev(c=1 - me.c)
    w3 = w4.reshape(TILES, D, 128)
    g3 = g4.reshape(TILES, D, 128)

    loads = {}
    for i, (name, src) in enumerate(zip(INPUTS, hbm)):
        cp = pltpu.make_async_copy(src, getattr(R, name), R.lsem.at[i])
        cp.start()
        loads[name] = cp

    barrier = pltpu.get_barrier_semaphore()
    greeted = 0
    for dev in [me.peer(*p)[0] for p in PEERS] + [me.step("x", d) for d in (1, 3)] + [me.far(*p) for p in FARS]:
        pl.semaphore_signal(barrier, inc=1, device_id=dev, device_id_type=MESH)
        greeted += 1
    for name, cp in loads.items():
        if name not in ("tok", "cot"):
            cp.wait()

    vec8 = jnp.concatenate([getattr(R, n)[...].astype(F32) for n in INPUTS[:7]] + [jnp.zeros((1, 6), F32)], axis=0).astype(BF16)
    R.small[...] = (
        nn(R.init[...], one_hot(iota((HEAD, 128), 0) == iota((HEAD, 128), 1)))
        + nn(R.rate[...], one_hot(iota((HEADS, 128), 0) + RATE0 == iota((HEADS, 128), 1)))
        + tn(vec8, one_hot(iota((8, 128), 0) + VEC0 == iota((8, 128), 1)))
    )
    bias_col = tt(one_hot(iota((HEADS, S), 0) + RATE0 == iota((HEADS, S), 1)), R.bias_rate[...])

    srcs = (R.wq, R.wk, R.wv, R.wo, R.wg, R.wu, R.wd, R.small)
    pkf, pk, rv, rv2, stf = R.pkf, R.pk, R.rv, R.rv2, R.stf
    pkf[0] = jnp.zeros((PROWS, 128), F32)
    for h in range(2):
        for xl in range(2):
            for y in range(4):
                i = 0
                for w in OUT_WAVES:
                    for n, t in enumerate(w.mine(h, xl, y)):
                        where = tile_source(w, h, t)
                        if where is not None and (y == 0 or n >= w.nx + w.nz):
                            a, col = where
                            pkf[0, pl.ds(6 * i, 6), :] = srcs[a][:, 128 * col : 128 * col + 128].astype(F32)
                        i += 1
                pk[h * 8 + xl * 4 + y] = pkf[0].astype(BF16)
    pl.semaphore_wait(barrier, greeted)
    peers = [me.peer(*p) for p in PEERS]
    firsts = send_all([(pk.at[slot], rv.at[me.s], dev) for dev, slot in peers], rv.at[pl.ds(0, 15)])
    rv[pl.ds(me.s, 1)] = pk[pl.ds(me.s, 1)]

    ones = jnp.where(iota((256, 256), 0) // HEAD == iota((256, 256), 1) // HEAD, 1.0 / HEAD, 0.0).astype(BF16)
    rowtok = iota((S, 1), 0)
    mask_r, seg_r = layout_rows(lens_ref, rowtok)
    lane = iota((1, 512), 1)
    ltok = lane // 64 * 16 + lane % 16
    _, seg_l = layout_rows(lens_ref, ltok)
    loads["tok"].wait()
    loads["cot"].wait()
    R.mcot[pl.ds(me.c, 1)] = (R.cot[...].astype(F32) * mask_r).astype(BF16)[None]
    mc_copy = send(R.mcot.at[me.c], R.mcot.at[me.c], other)

    firsts.wait_recv()
    for s in range(16):
        pkf[s] = rv[s].astype(F32)

    def unpack(w, i0):
        for i, t in enumerate(w.mine(me.c, me.xl, me.y)):
            for s in range(16):
                stf[pl.ds(6 * s, 6), :] = pkf[s, pl.ds(6 * (i0 + i), 6), :]
            w4[t, me.z, me.xh] = stf[...].astype(BF16)

    def gather(w, color):
        forward = steps_forward(w, color, False)
        sent = []
        for n, (axis, rect) in enumerate(w.chain(color, me)):
            at = me.coord(axis)
            mine, lo, hi = rect(at), rect((at + 3) % 4), rect((at + 1) % 4)
            now = [send(view(w4, mine), view(w4, mine), me.step(axis, d), "out") for d in ((1, 3) if n in forward else (1, 3, 2))]
            sent += now
            yield
            for cp in now:
                cp.wait_recv()
            if n in forward:
                now = [
                    send(view(w4, lo, 0), view(w4, lo, 0), me.step(axis, 1), "out"),
                    send(view(w4, hi, 1), view(w4, hi, 1), me.step(axis, 3), "out"),
                ]
                sent += now
                yield
                for cp in now:
                    cp.wait_recv()
        if not w.split:
            off, cnt = w.span(color)
            rect = (w.start(me.c) + off, cnt, ALL, ALL)
            a = send(view(w4, rect), view(w4, rect), other, "out")
            sent.append(a)
            yield
            a.wait_recv()
        for cp in sent:
            cp.wait_send()

    def go(*chains):
        for ch in chains:
            next(ch, None)

    def finish(*chains):
        live = list(chains)
        while live:
            for ch in list(live):
                try:
                    next(ch)
                except StopIteration:
                    live.remove(ch)

    unpack(ONE, 0)
    one_x, one_z = gather(ONE, "x"), gather(ONE, "z")
    three_z = gather(THREE, "z")
    two_x, two_z, two_y = gather(TWO, "x"), gather(TWO, "z"), gather(TWO, "y")
    go(one_x, one_z)
    unpack(THREE, ONE.per)
    unpack(TWO, ONE.per + THREE.per)
    go(two_y, two_x, two_z, three_z)
    go(one_x, one_z)
    go(two_y)
    go(one_x, one_z)
    go(two_y, two_x, two_z)
    go(one_x, one_z)
    go(two_y, three_z)
    go(one_x, one_z)
    firsts.wait_send()

    def wpair(t):
        return jnp.concatenate([w3[t], w3[t + 1]], axis=1)

    small = w3[TS]
    vsel = one_hot(iota((16, 128), 1) == iota((16, 128), 0) + VEC0)
    vecs = nt(vsel, small)
    norm_gain, init_bias, inner_gain, inner_bias, post_gain, post_bias, mlp_gain = (vecs[i : i + 1] for i in range(7))

    for i in range(4):
        rows = pl.ds(32 * i, 32)
        x = R.tok[rows, :].astype(F32)
        r = lax.rsqrt(jnp.mean(x * x, axis=-1, keepdims=True) + EPS)
        R.nrm[rows, :] = (x * r * norm_gain).astype(BF16)
    normed = R.nrm[...]
    for g in range(GROUPS):
        R.q[:, lanes(g)] = nn(normed, wpair(TQ + 2 * g))
        R.k[:, lanes(g)] = nn(normed, wpair(TK + 2 * g))
        R.v[:, lanes(g)] = nn(normed, wpair(TV + 2 * g))
    sig_t = jax.nn.sigmoid(tt(small, normed) + bias_col)
    rate_t = sig_t * (1.0 / HEAD)
    srow = iota((S, S), 0)
    is_rate = (srow >= RATE0) & (srow < RATE0 + HEADS)
    mask_tok, _ = layout_rows(lens_ref, iota((1, S), 1))
    live = jnp.where(is_rate, rate_t * mask_tok, 0.0)
    rate_sum = jnp.sum(live)
    rate_max = jnp.max(live)
    count = jnp.sum(mask_tok) * HEADS

    tsel = one_hot(iota((S, 512), 0) == ltok)
    rt_hi, rt_lo = split2(rate_t)
    rate_x = nn(rt_hi, tsel) + nn(rt_lo, tsel)
    lane_head = lane // 16 % 4
    jrow = iota((S, 512), 0)
    rate_lane = []
    for g in range(GROUPS):
        here = jrow == RATE0 + 4 * g + lane_head
        rate_lane.append(jnp.sum(jnp.where(here, rate_x, 0.0), axis=0, keepdims=True))
        sel = one_hot(here)
        R.rr[g] = tn(rt_hi, sel) + tn(rt_lo, sel)

    same = seg_r == seg_l
    rmb, rin = rowtok // 16, rowtok % 16
    lmb, lin = lane // 64, lane % 16

    def before():
        return jnp.where(same & (rmb > lmb), 1.0 / MINI, 0.0)

    def after():
        return jnp.where(same & (rmb < lmb), 1.0 / MINI, 0.0)

    def k2():
        return before() + jnp.where((rmb == lmb) & (lin <= rin), 1.0 / (rin + 1).astype(F32), 0.0)

    def k2t():
        return after() + jnp.where((rmb == lmb) & (rin <= lin), 1.0 / (lin + 1).astype(F32), 0.0)

    rep = one_hot(iota((S, 256), 0) == iota((S, 256), 1) % HEAD)
    b0c = init_bias - jnp.concatenate([nn(init_bias[:, 256 * g : 256 * g + 256].astype(BF16), ones) for g in range(GROUPS)], axis=1)
    diag = iota((256, 256), 0) // HEAD == iota((256, 256), 1) // HEAD
    gain2 = inner_gain * inner_gain

    def w0(g):
        wide = nn(w3[TS, 256 * g : 256 * g + 256, :], rep)
        wide = wide - jnp.mean(wide, axis=-1, keepdims=True)
        return split2(jnp.where(diag, wide, 0.0))

    R.u[...] = inner_gain * (inner_bias - R.v[...] + R.k[...])
    for g in range(GROUPS):
        gl = slice(256 * g, 256 * g + 256)
        kb, kl = split2(R.k[:, lanes(g)])
        qb, ql = split2(R.q[:, lanes(g)])
        for m in range(8):
            rows, here = pl.ds(64 * m, 64), slice(16 * m, 16 * m + 16)
            R.kbd[g, rows, :] = block_rows(kb[here])
            R.dbd[g, rows, :] = block_rows(kl[here])
            R.qbd[g, rows, :] = block_rows(qb[here])
        sc = nt(jnp.concatenate([kb, qb, ql], axis=0), R.kbd[g])
        sk = sc[:S] + 1.0
        R.skk[g] = sk
        R.sqk[g] = sc[S : 2 * S] + sc[2 * S :] + nt(qb, R.dbd[g]) + 1.0
        R.pm[g] = (sk * before() * rate_lane[g]).astype(BF16)
        R.pmt[g] = (sk * after() * R.rr[g]).astype(BF16)
        wh, wl = w0(g)
        zz = nn(jnp.concatenate([kb, qb, kl, ql], axis=0), wh)
        zl = nn(jnp.concatenate([kb, qb], axis=0), wl)
        R.zc[:, lanes(g)] = zz[:S] + zz[2 * S : 3 * S] + zl[:S] + b0c[:, gl]
        R.zq[:, lanes(g)] = zz[S : 2 * S] + zz[3 * S :] + zl[S:] + b0c[:, gl]

    def by_group(fn):
        return jnp.concatenate([fn(g, slice(256 * g, 256 * g + 256)) for g in range(GROUPS)], axis=1)

    def seg_mean(x):
        xb = x.astype(BF16)
        return by_group(lambda g, gl: nn(xb[:, gl], ones))

    def seg_mean2(x):
        n = x.shape[0]
        both = jnp.concatenate(split2(x), axis=0)
        r = by_group(lambda g, gl: nn(both[:, gl], ones))
        return r[:n] + r[n:]

    for m in range(8):
        rows = pl.ds(16 * m, 16)
        z = R.zc[rows, :]
        if m > 0:
            h = (m - 1) // 2 * 128
            if h > 0:
                z = z - by_group(lambda g, gl: nn(R.pm[g, rows, 0:h], R.gbd[g, 0:h, :]))
            z = z - by_group(lambda g, gl: nn(R.pm[g, rows, h : 64 * m], R.gbd[g, h : 64 * m, :]))
        uu = R.u[rows, :]
        gz = gain2 * z
        red = seg_mean2(jnp.concatenate([z * z, gz, gz * z, uu * z, uu], axis=0))
        var, r_gz, r_gzz, r_uz, r_u = (red[16 * i : 16 * i + 16] for i in range(5))
        s = lax.rsqrt(var + EPS)
        mg = s * r_gz
        mgg = s * s * r_gzz
        c = mgg + s * r_uz
        zh = z * s
        e = gain2 * zh + uu
        y = e - (mg + r_u) - zh * c
        gh, glow = split2(mask_r[16 * m : 16 * m + 16] * s * y)
        for g in range(GROUPS):
            R.gbd[g, pl.ds(64 * m, 64), :] = block_rows(gh[:, 256 * g : 256 * g + 256])
        R.gh[rows, :] = gh
        R.gl[rows, :] = glow
        R.zc[rows, :] = zh
        R.s1[rows, :] = s
        R.c1[rows, :] = c
        R.e1[rows, :] = e
        R.y1[rows, :] = y
        R.n1[rows, :] = mg
        R.n2[rows, :] = mgg
        if m == 3:
            go(two_x, two_z)
    for g in range(GROUPS):
        gl = slice(256 * g, 256 * g + 256)
        for m in range(8):
            R.dbd[g, pl.ds(64 * m, 64), :] = block_rows(R.gl[16 * m : 16 * m + 16, gl])
        ah, al = split2(R.sqk[g] * (k2() * rate_lane[g]))
        za = nn(jnp.concatenate([ah, al], axis=0), R.gbd[g])
        zb = R.zq[:, lanes(g)] - (za[:S] + za[S:] + nn(ah, R.dbd[g]))
        both = jnp.concatenate(split2(zb * zb), axis=0)
        var = nn(both, ones)
        s2 = lax.rsqrt(var[:S] + var[S:] + EPS)
        zh2 = zb * s2
        R.zq[:, lanes(g)] = zh2
        R.s2[:, lanes(g)] = s2
        R.mix[:, lanes(g)] = R.q[:, lanes(g)] + zh2 * inner_gain[:, gl] + inner_bias[:, gl]

    for i in range(4):
        rows = pl.ds(32 * i, 32)
        x = R.mix[rows, :]
        x = x - jnp.mean(x, axis=-1, keepdims=True)
        p_ = lax.rsqrt(jnp.mean(x * x, axis=-1, keepdims=True) + EPS)
        phat = x * p_
        R.mix[rows, :] = phat
        R.pscale[rows, :] = jnp.broadcast_to(p_, (32, 128))
        R.post[rows, :] = (phat * post_gain + post_bias).astype(BF16)
    pb = R.post[...]
    mc_copy.wait_recv()
    R.xt[1] = R.mcot[...].reshape(2 * S, D).T
    go(two_y)
    finish(three_z, one_x, one_z)

    def out_pair(g):
        return jnp.concatenate([w3[tile_out(2 * g)], w3[tile_out(2 * g + 1)]], axis=1)

    for g in range(GROUPS):
        R.hid[:, lanes(g)] = R.tok[:, lanes(g)].astype(F32) + nn(pb, out_pair(g))
    for i in range(4):
        rows = pl.ds(32 * i, 32)
        x = R.hid[rows, :]
        r = lax.rsqrt(jnp.mean(x * x, axis=-1, keepdims=True) + EPS)
        R.nrm2[pl.ds(me.c, 1), rows, :] = (x * r * mlp_gain).astype(BF16)[None]
    n2_copy = send(R.nrm2.at[me.c], R.nrm2.at[me.c], other)
    for t in PADS:
        g3[t] = jnp.zeros((D, 128), BF16)
    n2_copy.wait_recv()
    R.xt[0] = R.nrm2[...].reshape(2 * S, D).T
    finish(two_x, two_z, two_y)

    used = [0]

    def reduce(w, color):
        forward = steps_forward(w, color, True)
        off, cnt = w.span(color)
        sent = []
        if not w.split:
            landed = (0 if w is LAST else LAST.half) + off
            own = w.start(me.c) + off
            a = send(g4.at[pl.ds(w.start(1 - me.c) + off, cnt)], rc.at[pl.ds(landed, cnt)], other, "back")
            sent.append(a)
            yield
            a.wait_recv()

            def add_tile(t, carry):
                for z in range(4):
                    for xh in range(2):
                        g4[own + t, z, xh] = (g4[own + t, z, xh].astype(F32) + rc[landed + t, z, xh].astype(F32)).astype(BF16)
                return carry

            lax.fori_loop(0, cnt, add_tile, 0)
        for n, (axis, rect) in enumerate(reversed(w.chain(color, me))):
            at = me.coord(axis)
            size, place = blocks(rect(at))
            base = used[0]
            used[0] += 3 * size
            _, nt_, z, xh = rect(at)
            lead = (nt_,) + ((4,) if z is ALL else ()) + ((2,) if xh is ALL else ())

            def slot(i, half=None, base=base, size=size, lead=lead):
                rows = ALL if half is None else pl.ds(48 * half, 48)
                return land.at[pl.ds(base + i * size, size)].reshape(*lead, 96, 128).at[(ALL,) * len(lead) + (rows,)]

            right, left, far = rect((at + 1) % 4), rect((at + 3) % 4), rect((at + 2) % 4)
            if n in forward:
                now = [
                    send(view(g4, far, 0), slot(2, 0), me.step(axis, 1), "back"),
                    send(view(g4, far, 1), slot(2, 1), me.step(axis, 3), "back"),
                ]
                sent += now
                yield
                for cp in now:
                    cp.wait_recv()
                right_at, left_at = blocks(right)[1], blocks(left)[1]

                def add_far(i, carry, base=base, size=size, right_at=right_at, left_at=left_at):
                    for half, where in ((0, right_at), (1, left_at)):
                        p = where(i) + (pl.ds(48 * half, 48),)
                        g4[p] = (g4[p].astype(F32) + land[base + 2 * size + i, pl.ds(48 * half, 48)].astype(F32)).astype(BF16)
                    return carry

                lax.fori_loop(0, size, add_far, 0)
                now = [send(view(g4, right), slot(0), me.step(axis, 1), "back"), send(view(g4, left), slot(1), me.step(axis, 3), "back")]
            else:
                now = [
                    send(view(g4, right), slot(0), me.step(axis, 1), "back"),
                    send(view(g4, left), slot(1), me.step(axis, 3), "back"),
                    send(view(g4, far), slot(2), me.step(axis, 2), "back"),
                ]
            sent += now
            yield
            for cp in now:
                cp.wait_recv()
            terms = len(now)

            def add_mine(i, carry, base=base, size=size, place=place, terms=terms):
                p = place(i)
                total = g4[p].astype(F32)
                for k_ in range(terms):
                    total += land[base + k_ * size + i].astype(F32)
                g4[p] = total.astype(BF16)
                return carry

            lax.fori_loop(0, size, add_mine, 0)
        for cp in sent:
            cp.wait_send()

    back_y, back_z, back_x = reduce(FIRST, "y"), reduce(FIRST, "z"), reduce(FIRST, "x")

    x2, mc = R.nrm2[...].reshape(2 * S, D), R.mcot[...].reshape(2 * S, D)
    for j in reversed(range(4)):
        wg, wu, wd = (wpair(tile_mlp(j, kind)) for kind in range(3))
        gate, up, ac = nn(x2, wg), nn(x2, wu), nn(mc, wd)
        sg = jax.nn.sigmoid(gate)
        silu = gate * sg
        a = (silu * up).astype(BF16)
        gc = (ac * up * (sg * (1.0 + gate * (1.0 - sg)))).astype(BF16)
        uc = (ac * silu).astype(BF16)
        o_part = nt(a, wd).reshape(2, S, D)
        t_part = (nt(gc, wg) + nt(uc, wu)).reshape(2, S, D)
        if j == 3:
            R.o2[...] = o_part
            R.t2[...] = t_part
        else:
            R.o2[...] += o_part
            R.t2[...] += t_part
        for h in range(2):
            sl = slice(128 * h, 128 * h + 128)
            g3[tile_mlp(j, 0) + h] = nn(R.xt[0], gc[:, sl]).astype(BF16)
            g3[tile_mlp(j, 1) + h] = nn(R.xt[0], uc[:, sl]).astype(BF16)
            g3[tile_mlp(j, 2) + h] = nn(R.xt[1], a[:, sl]).astype(BF16)
        if j == 2:
            go(back_y)
        if j == 1:
            go(back_z)
    t_copy = send(R.t2.at[1 - me.c], R.t_in, other)
    go(back_x)
    o_copy = send(R.o2.at[1 - me.c], R.o_in, other)

    t_copy.wait_recv()
    g_mlp_gain = jnp.zeros((1, D), F32)
    for i in range(4):
        rows = pl.ds(32 * i, 32)
        mr = mask_r[32 * i : 32 * i + 32]
        x = R.hid[rows, :]
        r = lax.rsqrt(jnp.mean(x * x, axis=-1, keepdims=True) + EPS)
        u = x * r
        t = R.t2[pl.ds(me.c, 1), rows, :][0] + R.t_in[rows, :]
        g_mlp_gain += jnp.sum(t * u, axis=0, keepdims=True)
        c = t * mlp_gain
        h = mr * R.cot[rows, :].astype(F32) + r * (c - u * jnp.mean(c * u, axis=-1, keepdims=True))
        R.hcot[rows, :] = h
        R.bcot[rows, :] = h.astype(BF16)

    bc = R.bcot[...]
    pt_ = pb.T
    for c_ in range(6):
        g3[tile_out(c_)] = nn(pt_, bc[:, 128 * c_ : 128 * c_ + 128]).astype(BF16)
    go(back_y, back_z)
    acc = nt(bc[:, 0:256], out_pair(0))
    for g in range(1, GROUPS):
        acc += nt(bc[:, 256 * g : 256 * g + 256], out_pair(g))
    R.tcot[...] = acc
    go(back_x)
    o_copy.wait_recv()
    for i in range(4):
        rows = pl.ds(32 * i, 32)
        o = R.hid[rows, :] + R.o2[pl.ds(me.c, 1), rows, :][0] + R.o_in[rows, :]
        R.out[rows, :] = (mask_r[32 * i : 32 * i + 32] * o).astype(BF16)
    out_copy = pltpu.make_async_copy(R.out, out_any, R.lsem.at[0])
    out_copy.start()
    g_post_gain = jnp.zeros((1, D), F32)
    g_post_bias = jnp.zeros((1, D), F32)
    for i in range(4):
        rows = pl.ds(32 * i, 32)
        pc = R.tcot[rows, :]
        phat = R.mix[rows, :]
        g_post_gain += jnp.sum(pc * phat, axis=0, keepdims=True)
        g_post_bias += jnp.sum(pc, axis=0, keepdims=True)
        e = pc * post_gain
        R.tcot[rows, :] = R.pscale[rows, 0:1] * (
            e - jnp.mean(e, axis=-1, keepdims=True) - phat * jnp.mean(e * phat, axis=-1, keepdims=True)
        )

    do, zh2 = R.tcot[...], R.zq[...]
    g_inner_gain = jnp.sum(do * zh2, axis=0, keepdims=True)
    g_inner_bias = jnp.sum(do, axis=0, keepdims=True)
    dz = do * inner_gain
    dzb = R.s2[...] * (dz - zh2 * seg_mean(dz * zh2))
    gb_rows = jnp.sum(dzb, axis=0, keepdims=True)
    R.dzb[...] = dzb.astype(BF16)
    R.zbd[...] = jnp.zeros(R.zbd.shape, BF16)
    for g in range(GROUPS):
        db = R.dzb[:, lanes(g)]
        for m in range(8):
            R.dbd[g, pl.ds(64 * m, 64), :] = block_rows(db[16 * m : 16 * m + 16])
        kb = R.k[:, lanes(g)].astype(BF16)
        at = (nt(kb, R.qbd[g]) + 1.0) * (k2t() * R.rr[g])
        R.dgr[:, lanes(g)] = -nn(at.astype(BF16), R.dbd[g])

    for m in reversed(range(8)):
        rows = pl.ds(16 * m, 16)
        dg = R.dgr[rows, :]
        if m < 7:
            h = (m + 1) // 2 * 128
            if h + 128 < 512:
                dg = dg - by_group(lambda g, gl: nn(R.pmt[g, rows, h + 128 : 512], R.zbd[g, h + 128 : 512, :]))
            dg = dg - by_group(lambda g, gl: nn(R.pmt[g, rows, h : h + 128], R.zbd[g, h : h + 128, :]))
        hh = mask_r[16 * m : 16 * m + 16] * dg
        s, c, zh, e, y = R.s1[rows, :], R.c1[rows, :], R.zc[rows, :], R.e1[rows, :], R.y1[rows, :]
        zhh = zh * hh
        red = seg_mean(jnp.concatenate([hh, zhh, gain2 * zhh, y * hh], axis=0))
        m0, m1, m2, m3 = (red[16 * i : 16 * i + 16] for i in range(4))
        de = s * (hh - m0 - zh * m1)
        dzh = gain2 * de - s * (c * hh + e * m1)
        t = m2 - 2.0 * c * m1 - m0 * R.n1[rows, :] - m1 * R.n2[rows, :]
        dzc = s * (dzh - zh * (s * (m3 + t)))
        db = dzc.astype(BF16)
        for g in range(GROUPS):
            R.zbd[g, pl.ds(64 * m, 64), :] = block_rows(db[:, 256 * g : 256 * g + 256])
        R.dzc[rows, :] = db
        R.dgr[rows, :] = de
        R.dzf[rows, :] = dzc

    de = R.dgr[...]
    g_inner_gain += jnp.sum(de * (inner_bias - R.v[...] + R.k[...] + 2.0 * inner_gain * R.zc[...]), axis=0, keepdims=True)
    gde_all = inner_gain * de
    g_inner_bias += jnp.sum(gde_all, axis=0, keepdims=True)
    bsum = gb_rows + jnp.sum(R.dzf[...], axis=0, keepdims=True)
    g_init_bias = bsum - seg_mean2(jnp.broadcast_to(bsum, (16, D)))[0:1]
    x1t = R.nrm[...].T
    dv_all = (-gde_all).astype(BF16)
    for c_ in range(6):
        g3[TV + c_] = nn(x1t, dv_all[:, 128 * c_ : 128 * c_ + 128]).astype(BF16)
    mid_x, mid_z = reduce(MID, "x"), reduce(MID, "z")
    go(mid_x, mid_z)
    logit_acc = jnp.zeros((S, S), F32)
    wgrad_small = []
    for g in range(GROUPS):
        gl = slice(256 * g, 256 * g + 256)
        gde = inner_gain[:, gl] * R.dgr[:, lanes(g)]
        dzb_b, dzc_b = R.dzb[:, lanes(g)], R.dzc[:, lanes(g)]
        kb = R.k[:, lanes(g)].astype(BF16)
        qb = R.q[:, lanes(g)].astype(BF16)
        gb = R.gh[:, lanes(g)]
        rl, rr = rate_lane[g], R.rr[g]
        dd = nt(jnp.concatenate([dzb_b, dzc_b], axis=0), R.gbd[g])
        dr = -dd[:S] * k2()
        dp = -dd[S:] * before()
        drate = jnp.sum(dr * R.sqk[g] + dp * R.skk[g], axis=0, keepdims=True)
        dat = -nt(gb, R.dbd[g])
        dpt = -nt(gb, R.zbd[g])
        low = jnp.concatenate([(dr * rl).astype(BF16), (dp * rl + dpt * (after() * rr)).astype(BF16)], axis=0)
        dqk = nn(low, R.kbd[g])
        wh, _ = w0(g)
        dqk += nt(jnp.concatenate([dzb_b, dzc_b], axis=0), wh)
        dq = R.tcot[:, lanes(g)] + dqk[:S]
        dk = gde + dqk[S:] + nn((dat * (k2t() * rr)).astype(BF16), R.qbd[g])
        gwide = jnp.where(diag, tn(qb, dzb_b) + tn(kb, dzc_b), 0.0)
        fold = one_hot(iota((256, 128), 0) % HEAD == iota((256, 128), 1))
        gw_hi, gw_lo = split2(gwide)
        gsm = nn(gw_hi, fold) + nn(gw_lo, fold)
        wgrad_small.append(
            gsm - jnp.where(iota((256, 128), 1) < HEAD, jnp.sum(gsm, axis=-1, keepdims=True) * (1.0 / HEAD), 0.0)
        )
        dl = drate * rl * (1.0 - rl * HEAD)
        dlx = jnp.where(jrow == RATE0 + 4 * g + lane_head, dl, 0.0)
        logit_acc += nt(dlx.astype(BF16), tsel)
        dqb, dkb, dvb = dq.astype(BF16), dk.astype(BF16), (-gde).astype(BF16)
        for h in range(2):
            sl = slice(128 * h, 128 * h + 128)
            g3[TQ + 2 * g + h] = nn(x1t, dqb[:, sl]).astype(BF16)
            g3[TK + 2 * g + h] = nn(x1t, dkb[:, sl]).astype(BF16)
        part = nt(dqb, wpair(TQ + 2 * g)) + nt(dkb, wpair(TK + 2 * g)) + nt(dvb, wpair(TV + 2 * g))
        if g == 0:
            R.ot[...] = part
        else:
            R.ot[...] += part

    last_x, last_z = reduce(LAST, "x"), reduce(LAST, "z")
    go(last_x, mid_x, mid_z, back_y)
    logit_b = logit_acc.astype(BF16)
    oc_all = R.ot[...] + tt(logit_b, small)
    R.ot[...] = oc_all
    g_bias = jnp.sum(logit_acc, axis=1, keepdims=True)
    g_rate = nt(x1t, logit_b)
    g_norm_gain = jnp.zeros((1, D), F32)
    for i in range(4):
        rows = pl.ds(32 * i, 32)
        x = R.tok[rows, :].astype(F32)
        r = lax.rsqrt(jnp.mean(x * x, axis=-1, keepdims=True) + EPS)
        g_norm_gain += jnp.sum(R.ot[rows, :] * (x * r), axis=0, keepdims=True)

    vec_rows = jnp.concatenate(
        [g_norm_gain, g_init_bias, g_inner_gain, g_inner_bias, g_post_gain, g_post_bias, g_mlp_gain, jnp.zeros((9, D), F32)], axis=0
    ).astype(BF16)
    g3[TS] = (jnp.concatenate(wgrad_small, axis=0) + g_rate + tn(vec_rows, vsel)).astype(BF16)
    go(last_z)

    bias_row = jnp.sum(jnp.where(iota((S, S), 0) == iota((S, S), 1), g_bias, 0.0), axis=0, keepdims=True)
    r8 = iota((8, 128), 0)
    R.stat[...] = jnp.where(
        r8 == 0, rate_sum, jnp.where(r8 == 1, count, jnp.where(r8 == 2, rate_max, jnp.where(r8 == 3, bias_row, 0.0)))
    )
    stats = send_all([(R.stat, R.sa.at[me.s], dev) for dev, _ in peers], R.sa.at[pl.ds(0, 15)])
    R.sa[pl.ds(me.s, 1)] = R.stat[...][None]
    for i in range(4):
        rows = pl.ds(32 * i, 32)
        x = R.tok[rows, :].astype(F32)
        r = lax.rsqrt(jnp.mean(x * x, axis=-1, keepdims=True) + EPS)
        w = x * r
        f = R.ot[rows, :] * norm_gain
        R.gtok[rows, :] = (R.hcot[rows, :] + r * (f - w * jnp.mean(f * w, axis=-1, keepdims=True))).astype(BF16)
    gtok_copy = pltpu.make_async_copy(R.gtok, gtok_any, R.lsem.at[1])
    gtok_copy.start()

    go(last_x, back_z, back_x, last_z)

    def combine(buf, n):
        total, peak = buf[0], buf[0]
        for s in range(1, n):
            total, peak = total + buf[s], jnp.maximum(peak, buf[s])
        return jnp.where(r8 == 2, peak, total)

    stats.wait_recv()
    R.sb[pl.ds(me.zx, 1)] = combine(R.sa, 16)[None]
    stats2 = send_all([(R.sb.at[me.zx], R.sb.at[me.zx], me.far(*p)) for p in FARS], R.sb.at[pl.ds(0, 7)])
    finish(mid_x, mid_z, back_y, last_x, last_z, back_z, back_x)

    i = 0
    for w in BACK_WAVES:
        for t in w.mine(me.c, me.xl, me.y):
            stf[...] = g4[t, me.z, me.xh].astype(F32)
            for s in range(16):
                pkf[s, pl.ds(6 * i, 6), :] = stf[pl.ds(6 * s, 6), :]
            i += 1
    for s in range(16):
        pk[s] = pkf[s].astype(BF16)
    last = send_all([(pk.at[slot], rv2.at[me.s], dev) for dev, slot in peers], rv2.at[pl.ds(0, 15)])
    rv2[pl.ds(me.s, 1)] = pk[pl.ds(me.s, 1)]
    stats2.wait_recv()
    R.stat_sum[...] = combine(R.sb, 8)
    stat_copy = pltpu.make_async_copy(R.stat_sum, stat_any, R.lsem.at[2])
    stat_copy.start()
    last.wait_recv()
    raw_copy = pltpu.make_async_copy(rv2, raw_any, R.lsem.at[3])
    raw_copy.start()
    for cp in (mc_copy, n2_copy, t_copy, o_copy, stats, stats2, last):
        cp.wait_send()
    for cp in (out_copy, gtok_copy, stat_copy, raw_copy):
        cp.wait()


def step(lens, *arrays):
    anym = pl.BlockSpec(memory_space=pl.ANY)
    sd = jax.ShapeDtypeStruct
    return pl.pallas_call(
        step_kernel,
        out_shape=(sd((S, D), BF16), sd((S, D), BF16), sd((16, PROWS, 128), BF16), sd((8, 128), F32)),
        in_specs=[pl.BlockSpec(memory_space=pltpu.SMEM)] + [anym] * len(INPUTS),
        out_specs=(anym,) * 4,
        scratch_shapes=list(SCRATCH.values()),
        compiler_params=pltpu.CompilerParams(collective_id=0, has_side_effects=True, vmem_limit_bytes=60 * 2**20),
        name="step",
    )(lens, *arrays)


def finish_kernel(raw, stat, out_in, gtok_in, *outs):
    (out, gtok, g_norm, gq, gk, gv, g_rate, g_brate, g_init, g_ib, g_ig, g_ibias, g_pg, g_pb, go, g_mg, gg, gu, gd,
     r_mean, r_max, pkf) = outs
    out[...] = out_in[...]
    gtok[...] = gtok_in[...]
    mats = (gq, gk, gv, go, gg, gu, gd)
    for s in range(16):
        pkf[s] = raw[s].astype(F32)
    for h in range(2):
        for xl in range(2):
            i = 0
            for w in BACK_WAVES:
                for n in range(w.per):
                    for y in range(4 if n >= w.nx + w.nz else 1):
                        where = tile_source(w, h, w.mine(h, xl, y)[n])
                        if where is None:
                            continue
                        if n < w.nx + w.nz:
                            x = [pkf[h * 8 + xl * 4 + y_, pl.ds(6 * i, 6), :] for y_ in range(4)]
                            val = (x[0] + x[1]) + (x[2] + x[3])
                        else:
                            val = pkf[h * 8 + xl * 4 + y, pl.ds(6 * i, 6), :]
                        a, col = where
                        if a < A_S:
                            mats[a][:, 128 * col : 128 * col + 128] = val
                        else:
                            g_init[...] = val[:, :HEAD]
                            g_rate[...] = val[:, RATE0 : RATE0 + HEADS]
                            vt = val.T
                            for n_, ref in enumerate((g_norm, g_ib, g_ig, g_ibias, g_pg, g_pb, g_mg)):
                                ref[...] = vt[VEC0 + n_ : VEC0 + n_ + 1, :]
                    i += 1
    st = stat[...]
    g_brate[...] = st[3:4, RATE0 : RATE0 + HEADS]
    r_mean[...] = st[0:1, 0:1] / st[1:2, 0:1]
    r_max[...] = st[2:3, 0:1]


def finish_call(raw, stat, out, gtok):
    vm = pl.BlockSpec(memory_space=pltpu.VMEM)
    sd = jax.ShapeDtypeStruct
    row = sd((1, 6), F32)
    m768, m2048 = sd((6, 768), F32), sd((6, FF), F32)
    shapes = (
        sd((S, D), BF16), sd((S, D), BF16), row, m768, m768, m768, sd((6, HEADS), F32), sd((1, HEADS), F32),
        sd((6, HEAD), F32), row, row, row, row, row, m768, row, m2048, m2048, m2048, sd((1, 1), F32), sd((1, 1), F32),
    )
    return pl.pallas_call(
        finish_kernel, out_shape=shapes, in_specs=[vm] * 4, out_specs=(vm,) * 21,
        scratch_shapes=[pltpu.VMEM((16, PROWS, 128), F32)], name="finish",
    )(raw, stat, out, gtok)


def per_device(
    tokens, cotangent, seq_lengths, norm_gain, weight_query, weight_key, weight_value, weight_rate, bias_rate,
    init_weight, init_bias, inner_gain, inner_bias, post_gain, post_bias, weight_out, mlp_gain, weight_gate, weight_up,
    weight_down,
):
    rows = (norm_gain, init_bias, inner_gain, inner_bias, post_gain, post_bias, mlp_gain)
    out, gtok, raw, stat = step(
        seq_lengths, *[r.reshape(1, -1) for r in rows + (bias_rate,)], tokens, cotangent, weight_query, weight_key, weight_value, weight_out, weight_gate, weight_up,
        weight_down, init_weight, weight_rate,
    )
    res = list(finish_call(raw, stat, out, gtok))
    for i in (2, 9, 10, 11, 12, 13, 15):
        res[i] = res[i].reshape(6)
    res[7] = res[7].reshape(HEADS)
    res[19], res[20] = res[19].reshape(()), res[20].reshape(())
    return tuple(res)


def solution(mesh):
    both = ("dp", "sub")
    mat, vec, rep = P(both, None), P(both), P()
    return jax.shard_map(
        per_device,
        mesh=mesh,
        in_specs=(mat, mat, mat, vec, mat, mat, mat, mat, rep, mat, vec, vec, vec, vec, vec, mat, vec, mat, mat, mat),
        out_specs=(mat, mat, vec, mat, mat, mat, mat, rep, mat, vec, vec, vec, vec, vec, mat, vec, mat, mat, mat, rep, rep),
        check_vma=False,
    )
```

```python
import jax
import jax.numpy as jnp
from jax import lax
from jax.experimental import pallas as pl
from jax.experimental.pallas import tpu as pltpu
from jax.sharding import PartitionSpec as P

MESH = pl.DeviceIdType.MESH
HEADS = 12
HEAD = 64
MINI = 16
EPS = 1e-06
F32 = jnp.float32
BF16 = jnp.bfloat16
S = 128
D = 768
FF = 2048
GROUPS = 3
RATE0 = 64
VEC0 = 76
ALL = slice(None)


class Wave:
    def __init__(self, base, nx, nz, ny, split=False):
        self.base, self.nx, self.nz, self.ny = base, nx, nz, ny
        self.half = 2 * nx + 2 * nz + 8 * ny
        self.per = nx + nz + ny
        self.split = split

    def start(self, h):
        return self.base if self.split else self.base + h * self.half

    def tx(self, h, xl):
        return self.start(h) + xl * self.nx

    def tz(self, h, xl):
        return self.start(h) + 2 * self.nx + xl * self.nz

    def ty(self, h, y, xl):
        return self.start(h) + 2 * self.nx + 2 * self.nz + (y * 2 + xl) * self.ny

    def mine(self, h, xl, y):
        return (
            [self.tx(h, xl) + n for n in range(self.nx)]
            + [self.tz(h, xl) + n for n in range(self.nz)]
            + [self.ty(h, y, xl) + n for n in range(self.ny)]
        )

    def span(self, color):
        return {
            "x": (0, 2 * self.nx),
            "z": (2 * self.nx, 2 * self.nz),
            "y": (2 * self.nx + 2 * self.nz, 8 * self.ny),
        }[color]

    def chain(self, color, me):
        if color == "x":
            return [
                ("z", lambda p: (self.tx(me.c, me.xl), self.nx, p, me.xh)),
                ("x", lambda p: (self.tx(me.c, p % 2), self.nx, ALL, p // 2)),
            ]
        if color == "z":
            return [
                ("x", lambda p: (self.tz(me.c, p % 2), self.nz, me.z, p // 2)),
                ("z", lambda p: (self.tz(me.c, 0), 2 * self.nz, p, ALL)),
            ]
        return [
            ("z", lambda p: (self.ty(me.c, me.y, me.xl), self.ny, p, me.xh)),
            ("x", lambda p: (self.ty(me.c, me.y, p % 2), self.ny, ALL, p // 2)),
            ("y", lambda p: (self.ty(me.c, p, 0), 2 * self.ny, ALL, ALL)),
        ]

    def colors(self, order="xzy"):
        return [k for k in order if {"x": self.nx, "z": self.nz, "y": self.ny}[k]]


ONE, THREE, TWO = Wave(0, 3, 3, 0), Wave(24, 0, 1, 0), Wave(28, 4, 4, 1, split=True)
OUT_WAVES = (ONE, THREE, TWO)
LAST, MID, FIRST = Wave(0, 2, 2, 0), Wave(16, 1, 2, 0), Wave(28, 4, 4, 1, split=True)
BACK_WAVES = (LAST, MID, FIRST)
TILES = 52
PER = max(sum(w.per for w in ws) for ws in (OUT_WAVES, BACK_WAVES))
PROWS = (PER * 6 + 15) // 16 * 16
EARLY, LATE = BACK_WAVES[1:], BACK_WAVES[:1]


def rows_of(waves):
    return (sum(w.per for w in waves) * 6 + 15) // 16 * 16


TQ, TK, TS, TV = 0, 6, 12, 16
PADS = (25, 26, 27)
A_Q, A_K, A_V, A_O, A_G, A_U, A_D, A_S = range(8)
WIDTHS = (768, 768, 768, 768, 2048, 2048, 2048, 128)


def tile_out(c):
    return 13 + c if c < 3 else 19 + c


def tile_mlp(j, kind):
    return TWO.base + 6 * j + 2 * kind


def tile_source(w, h, t):
    if w.split:
        o = t - w.base
        return A_G + o % 6 // 2, 8 * h + o // 6 * 2 + o % 2
    if t in PADS:
        return None
    for a, first in ((A_Q, TQ), (A_K, TK), (A_V, TV)):
        if first <= t < first + 6:
            return a, t - first
    if t == TS:
        return A_S, 0
    return A_O, t - 13 if t < TV else t - 19


def nn(a, b):
    return lax.dot_general(a, b, (((1,), (0,)), ((), ())), preferred_element_type=F32)


def nt(a, b):
    return lax.dot_general(a, b, (((1,), (1,)), ((), ())), preferred_element_type=F32)


def tn(a, b):
    return lax.dot_general(a, b, (((0,), (0,)), ((), ())), preferred_element_type=F32)


def tt(a, b):
    return lax.dot_general(a, b, (((0,), (1,)), ((), ())), preferred_element_type=F32)


def iota(shape, dim):
    return lax.broadcasted_iota(jnp.int32, shape, dim)


def one_hot(cond):
    return jnp.where(cond, 1.0, 0.0).astype(BF16)


def split2(x):
    hi = x.astype(BF16)
    return hi, (x - hi.astype(F32)).astype(BF16)


def head_select(x, h):
    return jnp.where(iota(x.shape, 1) // HEAD == h, x, jnp.zeros_like(x))


def block_rows(x):
    return jnp.concatenate([head_select(x, h) for h in range(4)], axis=0)


def lanes(g):
    return pl.ds(256 * g, 256)


def layout_rows(lens_ref, token):
    mask = jnp.zeros(token.shape, F32)
    seg = jnp.zeros(token.shape, F32)
    start = jnp.int32(0)
    for j in range(4):
        n = lens_ref[0, j]
        mask += jnp.where((token >= start) & (token < start + n), 1.0, 0.0)
        seg += jnp.where((token >= start) & (n > 0), 1.0, 0.0)
        start += (n + 15) // 16 * 16
    return mask, seg


class Place:
    def __init__(self):
        dp, sub = lax.axis_index("dp"), lax.axis_index("sub")
        self.z = dp // 4
        self.xh = dp // 2 % 2
        self.c = dp % 2
        self.xl = sub // 4
        self.y = sub % 4
        self.x = self.xh * 2 + self.xl
        self.s = self.c * 8 + sub
        self.zx = self.z * 2 + self.xh

    def dev(self, z=None, x=None, y=None, c=None):
        z = self.z if z is None else z
        x = self.x if x is None else x
        y = self.y if y is None else y
        c = self.c if c is None else c
        return (z * 4 + x // 2 * 2 + c, x % 2 * 4 + y)

    def coord(self, axis):
        return getattr(self, axis)

    def step(self, axis, d):
        return self.dev(**{axis: (self.coord(axis) + d) % 4})

    def peer(self, dc, dxl, dy):
        c, xl, y = (self.c + dc) % 2, (self.xl + dxl) % 2, (self.y + dy) % 4
        return self.dev(x=self.xh * 2 + xl, y=y, c=c), c * 8 + xl * 4 + y

    def far(self, dz, dxh):
        return self.dev(z=(self.z + dz) % 4, x=(self.xh + dxh) % 2 * 2 + self.xl)


PEERS = tuple((dc, dxl, dy) for dc in range(2) for dxl in range(2) for dy in range(4) if (dc, dxl, dy) != (0, 0, 0))
FARS = tuple((dz, dxh) for dz in range(4) for dxh in range(2) if (dz, dxh) != (0, 0))


def blocks(rect):
    t, n, z, xh = rect
    nz, nxh = (4 if z is ALL else 1), (2 if xh is ALL else 1)

    def at(b):
        return (t + b // (nz * nxh), b // nxh % nz if z is ALL else z, b % nxh if xh is ALL else xh)

    return n * nz * nxh, at


def back_slots():
    slots = 0
    for w in BACK_WAVES:
        for color in w.colors():
            for _, rect in w.chain(color, Zero):
                slots += 3 * blocks(rect(0))[0]
    return slots


class Zero:
    z = xh = c = xl = y = x = s = 0


BACK_SLOTS = back_slots()


def steps_forward(w, color, back):
    if w.split:
        if back:
            return {"x": (0,), "z": (0,), "y": (0, 1)}[color]
        return {"x": (1,), "z": (1,), "y": (1, 2)}[color]
    if back:
        return (0,)
    return (1,) if w is ONE else ()


def copies_of(w, color, back):
    fwd = steps_forward(w, color, back)
    return sum(2 if n in fwd else 1 for n in range(len(w.chain(color, Zero)))) + (0 if w.split else 1 if back else 4)


OUT_COPIES = sum(copies_of(w, k, False) for w in OUT_WAVES for k in w.colors())
BACK_COPIES = sum(copies_of(w, k, True) for w in BACK_WAVES for k in w.colors())
RECV_SEMS = OUT_COPIES + BACK_COPIES + 8
SEND_SEMS = max(OUT_COPIES, BACK_COPIES) + 8


def view(ref, rect, half=None):
    t, n, z, xh = rect
    rows = ALL if half is None else pl.ds(48 * half, 48)
    return ref.at[pl.ds(t, n), z, xh, rows]


def f32(*shape):
    return pltpu.VMEM(shape, F32)


def b16(*shape):
    return pltpu.VMEM(shape, BF16)


INPUTS = ("norm_gain", "init_bias", "inner_gain", "inner_bias", "post_gain", "post_bias", "mlp_gain", "bias_rate", "tok", "cot",
          "wq", "wk", "wv", "wo", "wg", "wu", "wd", "init", "rate")
SCRATCH = dict(
    norm_gain=b16(1, 6), init_bias=b16(1, 6), inner_gain=b16(1, 6), inner_bias=b16(1, 6), post_gain=b16(1, 6), post_bias=b16(1, 6),
    mlp_gain=b16(1, 6), bias_rate=b16(1, HEADS), tok=b16(S, D), cot=b16(S, D), wq=b16(6, 768), wk=b16(6, 768), wv=b16(6, 768),
    wo=b16(6, 768), wg=b16(6, FF), wu=b16(6, FF), wd=b16(6, FF), init=b16(6, HEAD), rate=b16(6, HEADS), small=f32(6, 128),
    w4=b16(TILES, 4, 2, 96, 128), g4=b16(TILES, 4, 2, 96, 128), rc=b16(LAST.half + MID.half, 4, 2, 96, 128),
    land=b16(BACK_SLOTS, 96, 128), pk=b16(16, PROWS, 128), pkf=f32(16, PROWS, 128), rv=b16(16, PROWS, 128),
    pk_a=b16(16, rows_of(EARLY), 128), rv_a=b16(16, rows_of(EARLY), 128), pk_b=b16(16, rows_of(LATE), 128),
    rv_b=b16(16, rows_of(LATE), 128), stf=f32(96, 128), sa=f32(16, 8, 128), sb=f32(8, 8, 128), stat=f32(8, 128), stat_sum=f32(8, 128),
    nrm=b16(S, D), q=f32(S, D), k=f32(S, D), v=f32(S, D), zc=f32(S, D), zq=f32(S, D), u=f32(S, D), gh=b16(S, D), gl=b16(S, D),
    s1=f32(S, D), c1=f32(S, D), e1=f32(S, D), y1=f32(S, D), n1=f32(S, D), n2=f32(S, D), s2=f32(S, D),
    mix=f32(S, D), hid=f32(S, D), post=b16(S, D), dzb=b16(S, D), dzc=b16(S, D), dgr=f32(S, D), dzf=f32(S, D),
    kbd=b16(GROUPS, 512, 256), qbd=b16(GROUPS, 512, 256), gbd=b16(GROUPS, 512, 256), dbd=b16(GROUPS, 512, 256),
    zbd=b16(GROUPS, 512, 256), pm=b16(GROUPS, S, 512), pmt=b16(GROUPS, S, 512), skk=f32(GROUPS, S, 512), sqk=f32(GROUPS, S, 512),
    rr=f32(GROUPS, S, 512), pscale=f32(S, 128), hcot=f32(S, D), bcot=b16(S, D), tcot=f32(S, D), ot=f32(S, D), out=b16(S, D),
    gtok=b16(S, D),
    nrm2=b16(2, S, D), mcot=b16(2, S, D), xt=b16(2, D, 2 * S), t2=f32(2, S, D), o2=f32(2, S, D), t_in=f32(S, D), o_in=f32(S, D),
    lsem=pltpu.SemaphoreType.DMA((len(INPUTS),)), ssem=pltpu.SemaphoreType.DMA((SEND_SEMS,)), rsem=pltpu.SemaphoreType.DMA((RECV_SEMS,)),
)


class Refs:
    def __init__(self, refs):
        for name, ref in zip(SCRATCH, refs, strict=True):
            setattr(self, name, ref)


def step_kernel(*refs):
    lens_ref = refs[0]
    hbm = refs[1 : 1 + len(INPUTS)]
    out_any, gtok_any, raw_a, raw_b, stat_any = refs[1 + len(INPUTS) : 6 + len(INPUTS)]
    R = Refs(refs[6 + len(INPUTS) :])
    w4, g4, rc, land = R.w4, R.g4, R.rc, R.land
    me = Place()
    taken = {"group": 0, "out": 8, "back": 8}

    def copy(src, dst, dev, i, j):
        return pltpu.make_async_remote_copy(
            src_ref=src, dst_ref=dst, send_sem=R.ssem.at[i], recv_sem=R.rsem.at[j], device_id=dev, device_id_type=MESH
        )

    def send(src, dst, dev, kind="group"):
        i = taken[kind]
        taken[kind] += 1
        cp = copy(src, dst, dev, i, i + OUT_COPIES if kind == "back" else i)
        cp.start()
        return cp

    def send_all(triples, whole):
        i = taken["group"]
        taken["group"] += 1
        for src, dst, dev in triples:
            copy(src, dst, dev, i, i).start()
        return copy(whole, whole, me.dev(), i, i)

    other = me.dev(c=1 - me.c)
    w3 = w4.reshape(TILES, D, 128)
    g3 = g4.reshape(TILES, D, 128)

    loads = {}
    for i, (name, src) in enumerate(zip(INPUTS, hbm)):
        cp = pltpu.make_async_copy(src, getattr(R, name), R.lsem.at[i])
        cp.start()
        loads[name] = cp

    barrier = pltpu.get_barrier_semaphore()
    greeted = 0
    for dev in [me.peer(*p)[0] for p in PEERS] + [me.step("x", d) for d in (1, 3)] + [me.far(*p) for p in FARS]:
        pl.semaphore_signal(barrier, inc=1, device_id=dev, device_id_type=MESH)
        greeted += 1
    for name, cp in loads.items():
        if name not in ("tok", "cot"):
            cp.wait()

    vec8 = jnp.concatenate([getattr(R, n)[...].astype(F32) for n in INPUTS[:7]] + [jnp.zeros((1, 6), F32)], axis=0).astype(BF16)
    R.small[...] = (
        nn(R.init[...], one_hot(iota((HEAD, 128), 0) == iota((HEAD, 128), 1)))
        + nn(R.rate[...], one_hot(iota((HEADS, 128), 0) + RATE0 == iota((HEADS, 128), 1)))
        + tn(vec8, one_hot(iota((8, 128), 0) + VEC0 == iota((8, 128), 1)))
    )
    bias_col = tt(one_hot(iota((HEADS, S), 0) + RATE0 == iota((HEADS, S), 1)), R.bias_rate[...])

    srcs = (R.wq, R.wk, R.wv, R.wo, R.wg, R.wu, R.wd, R.small)
    pkf, pk, rv, stf = R.pkf, R.pk, R.rv, R.stf
    pkf[0] = jnp.zeros((PROWS, 128), F32)
    for h in range(2):
        for xl in range(2):
            for y in range(4):
                i = 0
                for w in OUT_WAVES:
                    for n, t in enumerate(w.mine(h, xl, y)):
                        where = tile_source(w, h, t)
                        if where is not None and (y == 0 or n >= w.nx + w.nz):
                            a, col = where
                            pkf[0, pl.ds(6 * i, 6), :] = srcs[a][:, 128 * col : 128 * col + 128].astype(F32)
                        i += 1
                pk[h * 8 + xl * 4 + y] = pkf[0].astype(BF16)
    pl.semaphore_wait(barrier, greeted)
    def send_step(triples, size, kind):
        i = taken[kind]
        taken[kind] += 1
        j = i + OUT_COPIES if kind == "back" else i
        for src, dst, dev in triples:
            copy(src, dst, dev, i, j).start()
        whole = land.at[pl.ds(0, size)]
        return copy(whole, whole, me.dev(), i, j)

    peers = [me.peer(*p) for p in PEERS]
    firsts = send_all([(pk.at[slot], rv.at[me.s], dev) for dev, slot in peers], rv.at[pl.ds(0, 15)])
    rv[pl.ds(me.s, 1)] = pk[pl.ds(me.s, 1)]

    ones = jnp.where(iota((256, 256), 0) // HEAD == iota((256, 256), 1) // HEAD, 1.0 / HEAD, 0.0).astype(BF16)
    rowtok = iota((S, 1), 0)
    mask_r, seg_r = layout_rows(lens_ref, rowtok)
    lane = iota((1, 512), 1)
    ltok = lane // 64 * 16 + lane % 16
    _, seg_l = layout_rows(lens_ref, ltok)
    loads["tok"].wait()
    loads["cot"].wait()
    R.mcot[pl.ds(me.c, 1)] = (R.cot[...].astype(F32) * mask_r).astype(BF16)[None]
    mc_copy = send(R.mcot.at[me.c], R.mcot.at[me.c], other)

    firsts.wait_recv()
    for s in range(16):
        pkf[s] = rv[s].astype(F32)

    def unpack(w, i0):
        for i, t in enumerate(w.mine(me.c, me.xl, me.y)):
            for s in range(16):
                stf[pl.ds(6 * s, 6), :] = pkf[s, pl.ds(6 * (i0 + i), 6), :]
            w4[t, me.z, me.xh] = stf[...].astype(BF16)

    def gather(w, color):
        forward = steps_forward(w, color, False)
        sent, crossed = [], []
        chain = w.chain(color, me)
        for n, (axis, rect) in enumerate(chain):
            at = me.coord(axis)
            mine, lo, hi, far = (rect((at + d) % 4) for d in (0, 3, 1, 2))
            last = n == len(chain) - 1 and not w.split

            def cross(*rects, last=last):
                if last:
                    crossed.extend(send(view(w4, r), view(w4, r), other, "out") for r in rects)

            size = blocks(mine)[0]
            where = (1, 3) if n in forward else (1, 3, 2)
            now = send_step([(view(w4, mine), view(w4, mine), me.step(axis, d)) for d in where], len(where) * size, "out")
            sent.append(now)
            cross(mine)
            yield
            now.wait_recv()
            if n in forward:
                now = send_step(
                    [(view(w4, lo, 0), view(w4, lo, 0), me.step(axis, 1)), (view(w4, hi, 1), view(w4, hi, 1), me.step(axis, 3))],
                    size, "out",
                )
                sent.append(now)
                cross(lo, hi)
                yield
                now.wait_recv()
                cross(far)
            else:
                cross(lo, hi, far)
        if crossed:
            yield
            for cp in crossed:
                cp.wait_recv()
        for cp in sent + crossed:
            cp.wait_send()

    def go(*chains):
        for ch in chains:
            next(ch, None)

    def finish(*chains):
        live = list(chains)
        while live:
            for ch in list(live):
                try:
                    next(ch)
                except StopIteration:
                    live.remove(ch)

    unpack(ONE, 0)
    one_x, one_z = gather(ONE, "x"), gather(ONE, "z")
    three_z = gather(THREE, "z")
    two_x, two_z, two_y = gather(TWO, "x"), gather(TWO, "z"), gather(TWO, "y")
    go(one_x, one_z)
    unpack(THREE, ONE.per)
    unpack(TWO, ONE.per + THREE.per)
    go(two_y, two_x, two_z, three_z)
    go(one_x, one_z)
    go(two_y)
    go(one_x, one_z)
    go(two_y, two_x, two_z)
    go(one_x, one_z)
    go(two_y, three_z)
    go(one_x, one_z)
    firsts.wait_send()

    def wpair(t):
        return jnp.concatenate([w3[t], w3[t + 1]], axis=1)

    small = w3[TS]
    vsel = one_hot(iota((16, 128), 1) == iota((16, 128), 0) + VEC0)
    vecs = nt(vsel, small)
    norm_gain, init_bias, inner_gain, inner_bias, post_gain, post_bias, mlp_gain = (vecs[i : i + 1] for i in range(7))

    for i in range(4):
        rows = pl.ds(32 * i, 32)
        x = R.tok[rows, :].astype(F32)
        r = lax.rsqrt(jnp.mean(x * x, axis=-1, keepdims=True) + EPS)
        R.nrm[rows, :] = (x * r * norm_gain).astype(BF16)
    normed = R.nrm[...]
    for g in range(GROUPS):
        R.q[:, lanes(g)] = nn(normed, wpair(TQ + 2 * g))
        R.k[:, lanes(g)] = nn(normed, wpair(TK + 2 * g))
        R.v[:, lanes(g)] = nn(normed, wpair(TV + 2 * g))
    sig_t = jax.nn.sigmoid(tt(small, normed) + bias_col)
    rate_t = sig_t * (1.0 / HEAD)
    srow = iota((S, S), 0)
    is_rate = (srow >= RATE0) & (srow < RATE0 + HEADS)
    mask_tok, _ = layout_rows(lens_ref, iota((1, S), 1))
    live = jnp.where(is_rate, rate_t * mask_tok, 0.0)
    rate_sum = jnp.sum(live)
    rate_max = jnp.max(live)
    count = jnp.sum(mask_tok) * HEADS

    tsel = one_hot(iota((S, 512), 0) == ltok)
    rt_hi, rt_lo = split2(rate_t)
    rate_x = nn(rt_hi, tsel) + nn(rt_lo, tsel)
    lane_head = lane // 16 % 4
    jrow = iota((S, 512), 0)
    rate_lane = []
    for g in range(GROUPS):
        here = jrow == RATE0 + 4 * g + lane_head
        rate_lane.append(jnp.sum(jnp.where(here, rate_x, 0.0), axis=0, keepdims=True))
        sel = one_hot(here)
        R.rr[g] = tn(rt_hi, sel) + tn(rt_lo, sel)

    same = seg_r == seg_l
    rmb, rin = rowtok // 16, rowtok % 16
    lmb, lin = lane // 64, lane % 16

    def before():
        return jnp.where(same & (rmb > lmb), 1.0 / MINI, 0.0)

    def after():
        return jnp.where(same & (rmb < lmb), 1.0 / MINI, 0.0)

    def k2():
        return before() + jnp.where((rmb == lmb) & (lin <= rin), 1.0 / (rin + 1).astype(F32), 0.0)

    def k2t():
        return after() + jnp.where((rmb == lmb) & (rin <= lin), 1.0 / (lin + 1).astype(F32), 0.0)

    rep = one_hot(iota((S, 256), 0) == iota((S, 256), 1) % HEAD)
    b0c = init_bias - jnp.concatenate([nn(init_bias[:, 256 * g : 256 * g + 256].astype(BF16), ones) for g in range(GROUPS)], axis=1)
    diag = iota((256, 256), 0) // HEAD == iota((256, 256), 1) // HEAD
    gain2 = inner_gain * inner_gain

    def w0(g):
        wide = nn(w3[TS, 256 * g : 256 * g + 256, :], rep)
        wide = wide - jnp.mean(wide, axis=-1, keepdims=True)
        return split2(jnp.where(diag, wide, 0.0))

    R.u[...] = inner_gain * (inner_bias - R.v[...] + R.k[...])
    for g in range(GROUPS):
        gl = slice(256 * g, 256 * g + 256)
        kb, kl = split2(R.k[:, lanes(g)])
        qb, ql = split2(R.q[:, lanes(g)])
        for m in range(8):
            rows, here = pl.ds(64 * m, 64), slice(16 * m, 16 * m + 16)
            R.kbd[g, rows, :] = block_rows(kb[here])
            R.dbd[g, rows, :] = block_rows(kl[here])
            R.qbd[g, rows, :] = block_rows(qb[here])
        sc = nt(jnp.concatenate([kb, qb, ql], axis=0), R.kbd[g])
        sk = sc[:S] + 1.0
        R.skk[g] = sk
        R.sqk[g] = sc[S : 2 * S] + sc[2 * S :] + nt(qb, R.dbd[g]) + 1.0
        R.pm[g] = (sk * before() * rate_lane[g]).astype(BF16)
        R.pmt[g] = (sk * after() * R.rr[g]).astype(BF16)
        wh, wl = w0(g)
        zz = nn(jnp.concatenate([kb, qb, kl, ql], axis=0), wh)
        zl = nn(jnp.concatenate([kb, qb], axis=0), wl)
        R.zc[:, lanes(g)] = zz[:S] + zz[2 * S : 3 * S] + zl[:S] + b0c[:, gl]
        R.zq[:, lanes(g)] = zz[S : 2 * S] + zz[3 * S :] + zl[S:] + b0c[:, gl]

    def by_group(fn):
        return jnp.concatenate([fn(g, slice(256 * g, 256 * g + 256)) for g in range(GROUPS)], axis=1)

    def seg_mean(x):
        xb = x.astype(BF16)
        return by_group(lambda g, gl: nn(xb[:, gl], ones))

    def seg_mean2(x):
        n = x.shape[0]
        both = jnp.concatenate(split2(x), axis=0)
        r = by_group(lambda g, gl: nn(both[:, gl], ones))
        return r[:n] + r[n:]

    for m in range(8):
        rows = pl.ds(16 * m, 16)
        z = R.zc[rows, :]
        if m > 0:
            h = (m - 1) // 2 * 128
            if h > 0:
                z = z - by_group(lambda g, gl: nn(R.pm[g, rows, 0:h], R.gbd[g, 0:h, :]))
            z = z - by_group(lambda g, gl: nn(R.pm[g, rows, h : 64 * m], R.gbd[g, h : 64 * m, :]))
        uu = R.u[rows, :]
        gz = gain2 * z
        red = seg_mean2(jnp.concatenate([z * z, gz, gz * z, uu * z, uu], axis=0))
        var, r_gz, r_gzz, r_uz, r_u = (red[16 * i : 16 * i + 16] for i in range(5))
        s = lax.rsqrt(var + EPS)
        mg = s * r_gz
        mgg = s * s * r_gzz
        c = mgg + s * r_uz
        zh = z * s
        e = gain2 * zh + uu
        y = e - (mg + r_u) - zh * c
        gh, glow = split2(mask_r[16 * m : 16 * m + 16] * s * y)
        for g in range(GROUPS):
            R.gbd[g, pl.ds(64 * m, 64), :] = block_rows(gh[:, 256 * g : 256 * g + 256])
        R.gh[rows, :] = gh
        R.gl[rows, :] = glow
        R.zc[rows, :] = zh
        R.s1[rows, :] = s
        R.c1[rows, :] = c
        R.e1[rows, :] = e
        R.y1[rows, :] = y
        R.n1[rows, :] = mg
        R.n2[rows, :] = mgg
        if m == 3:
            go(two_x, two_z)
    for g in range(GROUPS):
        gl = slice(256 * g, 256 * g + 256)
        for m in range(8):
            R.dbd[g, pl.ds(64 * m, 64), :] = block_rows(R.gl[16 * m : 16 * m + 16, gl])
        ah, al = split2(R.sqk[g] * (k2() * rate_lane[g]))
        za = nn(jnp.concatenate([ah, al], axis=0), R.gbd[g])
        zb = R.zq[:, lanes(g)] - (za[:S] + za[S:] + nn(ah, R.dbd[g]))
        both = jnp.concatenate(split2(zb * zb), axis=0)
        var = nn(both, ones)
        s2 = lax.rsqrt(var[:S] + var[S:] + EPS)
        zh2 = zb * s2
        R.zq[:, lanes(g)] = zh2
        R.s2[:, lanes(g)] = s2
        R.mix[:, lanes(g)] = R.q[:, lanes(g)] + zh2 * inner_gain[:, gl] + inner_bias[:, gl]

    for i in range(4):
        rows = pl.ds(32 * i, 32)
        x = R.mix[rows, :]
        x = x - jnp.mean(x, axis=-1, keepdims=True)
        p_ = lax.rsqrt(jnp.mean(x * x, axis=-1, keepdims=True) + EPS)
        phat = x * p_
        R.mix[rows, :] = phat
        R.pscale[rows, :] = jnp.broadcast_to(p_, (32, 128))
        R.post[rows, :] = (phat * post_gain + post_bias).astype(BF16)
    pb = R.post[...]
    mc_copy.wait_recv()
    R.xt[1] = R.mcot[...].reshape(2 * S, D).T
    go(two_y)
    finish(three_z, one_x, one_z)

    def out_pair(g):
        return jnp.concatenate([w3[tile_out(2 * g)], w3[tile_out(2 * g + 1)]], axis=1)

    for g in range(GROUPS):
        R.hid[:, lanes(g)] = R.tok[:, lanes(g)].astype(F32) + nn(pb, out_pair(g))
    for i in range(4):
        rows = pl.ds(32 * i, 32)
        x = R.hid[rows, :]
        r = lax.rsqrt(jnp.mean(x * x, axis=-1, keepdims=True) + EPS)
        R.nrm2[pl.ds(me.c, 1), rows, :] = (x * r * mlp_gain).astype(BF16)[None]
    n2_copy = send(R.nrm2.at[me.c], R.nrm2.at[me.c], other)
    for t in PADS:
        g3[t] = jnp.zeros((D, 128), BF16)
    n2_copy.wait_recv()
    R.xt[0] = R.nrm2[...].reshape(2 * S, D).T
    finish(two_x, two_z, two_y)

    used = [0]

    def reduce(w, color):
        forward = steps_forward(w, color, True)
        off, cnt = w.span(color)
        sent = []
        if not w.split:
            landed = (0 if w is LAST else LAST.half) + off
            own = w.start(me.c) + off
            a = send(g4.at[pl.ds(w.start(1 - me.c) + off, cnt)], rc.at[pl.ds(landed, cnt)], other, "back")
            sent.append(a)
            yield
            a.wait_recv()

            def add_tile(t, carry):
                for z in range(4):
                    for xh in range(2):
                        g4[own + t, z, xh] = (g4[own + t, z, xh].astype(F32) + rc[landed + t, z, xh].astype(F32)).astype(BF16)
                return carry

            lax.fori_loop(0, cnt, add_tile, 0)
        for n, (axis, rect) in enumerate(reversed(w.chain(color, me))):
            at = me.coord(axis)
            size, place = blocks(rect(at))
            base = used[0]
            used[0] += 3 * size
            _, nt_, z, xh = rect(at)
            lead = (nt_,) + ((4,) if z is ALL else ()) + ((2,) if xh is ALL else ())

            def slot(i, half=None, base=base, size=size, lead=lead):
                rows = ALL if half is None else pl.ds(48 * half, 48)
                return land.at[pl.ds(base + i * size, size)].reshape(*lead, 96, 128).at[(ALL,) * len(lead) + (rows,)]

            right, left, far = rect((at + 1) % 4), rect((at + 3) % 4), rect((at + 2) % 4)
            if n in forward:
                now = send_step(
                    [(view(g4, far, 0), slot(2, 0), me.step(axis, 1)), (view(g4, far, 1), slot(2, 1), me.step(axis, 3))],
                    size, "back",
                )
                sent.append(now)
                yield
                now.wait_recv()
                right_at, left_at = blocks(right)[1], blocks(left)[1]

                def add_far(i, carry, base=base, size=size, right_at=right_at, left_at=left_at):
                    for half, where in ((0, right_at), (1, left_at)):
                        p = where(i) + (pl.ds(48 * half, 48),)
                        g4[p] = (g4[p].astype(F32) + land[base + 2 * size + i, pl.ds(48 * half, 48)].astype(F32)).astype(BF16)
                    return carry

                lax.fori_loop(0, size, add_far, 0)
            triples = [(view(g4, right), slot(0), me.step(axis, 1)), (view(g4, left), slot(1), me.step(axis, 3))]
            if n not in forward:
                triples.append((view(g4, far), slot(2), me.step(axis, 2)))
            terms = len(triples)
            now = send_step(triples, terms * size, "back")
            sent.append(now)
            yield
            now.wait_recv()

            def add_mine(i, carry, base=base, size=size, place=place, terms=terms):
                p = place(i)
                total = g4[p].astype(F32)
                for k_ in range(terms):
                    total += land[base + k_ * size + i].astype(F32)
                g4[p] = total.astype(BF16)
                return carry

            lax.fori_loop(0, size, add_mine, 0)
        for cp in sent:
            cp.wait_send()

    back_y, back_z, back_x = reduce(FIRST, "y"), reduce(FIRST, "z"), reduce(FIRST, "x")

    x2, mc = R.nrm2[...].reshape(2 * S, D), R.mcot[...].reshape(2 * S, D)
    for j in reversed(range(4)):
        wg, wu, wd = (wpair(tile_mlp(j, kind)) for kind in range(3))
        gate, up, ac = nn(x2, wg), nn(x2, wu), nn(mc, wd)
        sg = jax.nn.sigmoid(gate)
        silu = gate * sg
        a = (silu * up).astype(BF16)
        gc = (ac * up * (sg * (1.0 + gate * (1.0 - sg)))).astype(BF16)
        uc = (ac * silu).astype(BF16)
        o_part = nt(a, wd).reshape(2, S, D)
        t_part = (nt(gc, wg) + nt(uc, wu)).reshape(2, S, D)
        if j == 3:
            R.o2[...] = o_part
            R.t2[...] = t_part
        else:
            R.o2[...] += o_part
            R.t2[...] += t_part
        for h in range(2):
            sl = slice(128 * h, 128 * h + 128)
            g3[tile_mlp(j, 0) + h] = nn(R.xt[0], gc[:, sl]).astype(BF16)
            g3[tile_mlp(j, 1) + h] = nn(R.xt[0], uc[:, sl]).astype(BF16)
            g3[tile_mlp(j, 2) + h] = nn(R.xt[1], a[:, sl]).astype(BF16)
        if j == 2:
            go(back_y)
        if j == 1:
            go(back_z)
    t_copy = send(R.t2.at[1 - me.c], R.t_in, other)
    go(back_x)
    o_copy = send(R.o2.at[1 - me.c], R.o_in, other)

    t_copy.wait_recv()
    g_mlp_gain = jnp.zeros((1, D), F32)
    for i in range(4):
        rows = pl.ds(32 * i, 32)
        mr = mask_r[32 * i : 32 * i + 32]
        x = R.hid[rows, :]
        r = lax.rsqrt(jnp.mean(x * x, axis=-1, keepdims=True) + EPS)
        u = x * r
        t = R.t2[pl.ds(me.c, 1), rows, :][0] + R.t_in[rows, :]
        g_mlp_gain += jnp.sum(t * u, axis=0, keepdims=True)
        c = t * mlp_gain
        h = mr * R.cot[rows, :].astype(F32) + r * (c - u * jnp.mean(c * u, axis=-1, keepdims=True))
        R.hcot[rows, :] = h
        R.bcot[rows, :] = h.astype(BF16)

    bc = R.bcot[...]
    pt_ = pb.T
    for c_ in range(6):
        g3[tile_out(c_)] = nn(pt_, bc[:, 128 * c_ : 128 * c_ + 128]).astype(BF16)
    go(back_y, back_z)
    acc = nt(bc[:, 0:256], out_pair(0))
    for g in range(1, GROUPS):
        acc += nt(bc[:, 256 * g : 256 * g + 256], out_pair(g))
    R.tcot[...] = acc
    go(back_x)
    o_copy.wait_recv()
    for i in range(4):
        rows = pl.ds(32 * i, 32)
        o = R.hid[rows, :] + R.o2[pl.ds(me.c, 1), rows, :][0] + R.o_in[rows, :]
        R.out[rows, :] = (mask_r[32 * i : 32 * i + 32] * o).astype(BF16)
    out_copy = pltpu.make_async_copy(R.out, out_any, R.lsem.at[0])
    out_copy.start()
    g_post_gain = jnp.zeros((1, D), F32)
    g_post_bias = jnp.zeros((1, D), F32)
    for i in range(4):
        rows = pl.ds(32 * i, 32)
        pc = R.tcot[rows, :]
        phat = R.mix[rows, :]
        g_post_gain += jnp.sum(pc * phat, axis=0, keepdims=True)
        g_post_bias += jnp.sum(pc, axis=0, keepdims=True)
        e = pc * post_gain
        R.tcot[rows, :] = R.pscale[rows, 0:1] * (
            e - jnp.mean(e, axis=-1, keepdims=True) - phat * jnp.mean(e * phat, axis=-1, keepdims=True)
        )

    do, zh2 = R.tcot[...], R.zq[...]
    g_inner_gain = jnp.sum(do * zh2, axis=0, keepdims=True)
    g_inner_bias = jnp.sum(do, axis=0, keepdims=True)
    dz = do * inner_gain
    dzb = R.s2[...] * (dz - zh2 * seg_mean(dz * zh2))
    gb_rows = jnp.sum(dzb, axis=0, keepdims=True)
    R.dzb[...] = dzb.astype(BF16)
    R.zbd[...] = jnp.zeros(R.zbd.shape, BF16)
    for g in range(GROUPS):
        db = R.dzb[:, lanes(g)]
        for m in range(8):
            R.dbd[g, pl.ds(64 * m, 64), :] = block_rows(db[16 * m : 16 * m + 16])
        kb = R.k[:, lanes(g)].astype(BF16)
        at = (nt(kb, R.qbd[g]) + 1.0) * (k2t() * R.rr[g])
        R.dgr[:, lanes(g)] = -nn(at.astype(BF16), R.dbd[g])

    for m in reversed(range(8)):
        rows = pl.ds(16 * m, 16)
        dg = R.dgr[rows, :]
        if m < 7:
            h = (m + 1) // 2 * 128
            if h + 128 < 512:
                dg = dg - by_group(lambda g, gl: nn(R.pmt[g, rows, h + 128 : 512], R.zbd[g, h + 128 : 512, :]))
            dg = dg - by_group(lambda g, gl: nn(R.pmt[g, rows, h : h + 128], R.zbd[g, h : h + 128, :]))
        hh = mask_r[16 * m : 16 * m + 16] * dg
        s, c, zh, e, y = R.s1[rows, :], R.c1[rows, :], R.zc[rows, :], R.e1[rows, :], R.y1[rows, :]
        zhh = zh * hh
        red = seg_mean(jnp.concatenate([hh, zhh, gain2 * zhh, y * hh], axis=0))
        m0, m1, m2, m3 = (red[16 * i : 16 * i + 16] for i in range(4))
        de = s * (hh - m0 - zh * m1)
        dzh = gain2 * de - s * (c * hh + e * m1)
        t = m2 - 2.0 * c * m1 - m0 * R.n1[rows, :] - m1 * R.n2[rows, :]
        dzc = s * (dzh - zh * (s * (m3 + t)))
        db = dzc.astype(BF16)
        for g in range(GROUPS):
            R.zbd[g, pl.ds(64 * m, 64), :] = block_rows(db[:, 256 * g : 256 * g + 256])
        R.dzc[rows, :] = db
        R.dgr[rows, :] = de
        R.dzf[rows, :] = dzc

    de = R.dgr[...]
    g_inner_gain += jnp.sum(de * (inner_bias - R.v[...] + R.k[...] + 2.0 * inner_gain * R.zc[...]), axis=0, keepdims=True)
    gde_all = inner_gain * de
    g_inner_bias += jnp.sum(gde_all, axis=0, keepdims=True)
    bsum = gb_rows + jnp.sum(R.dzf[...], axis=0, keepdims=True)
    g_init_bias = bsum - seg_mean2(jnp.broadcast_to(bsum, (16, D)))[0:1]
    x1t = R.nrm[...].T
    dv_all = (-gde_all).astype(BF16)
    for c_ in range(6):
        g3[TV + c_] = nn(x1t, dv_all[:, 128 * c_ : 128 * c_ + 128]).astype(BF16)
    mid_x, mid_z = reduce(MID, "x"), reduce(MID, "z")
    go(mid_x, mid_z)
    logit_acc = jnp.zeros((S, S), F32)
    wgrad_small = []
    for g in range(GROUPS):
        gl = slice(256 * g, 256 * g + 256)
        gde = inner_gain[:, gl] * R.dgr[:, lanes(g)]
        dzb_b, dzc_b = R.dzb[:, lanes(g)], R.dzc[:, lanes(g)]
        kb = R.k[:, lanes(g)].astype(BF16)
        qb = R.q[:, lanes(g)].astype(BF16)
        gb = R.gh[:, lanes(g)]
        rl, rr = rate_lane[g], R.rr[g]
        dd = nt(jnp.concatenate([dzb_b, dzc_b], axis=0), R.gbd[g])
        dr = -dd[:S] * k2()
        dp = -dd[S:] * before()
        drate = jnp.sum(dr * R.sqk[g] + dp * R.skk[g], axis=0, keepdims=True)
        dat = -nt(gb, R.dbd[g])
        dpt = -nt(gb, R.zbd[g])
        low = jnp.concatenate([(dr * rl).astype(BF16), (dp * rl + dpt * (after() * rr)).astype(BF16)], axis=0)
        dqk = nn(low, R.kbd[g])
        wh, _ = w0(g)
        dqk += nt(jnp.concatenate([dzb_b, dzc_b], axis=0), wh)
        dq = R.tcot[:, lanes(g)] + dqk[:S]
        dk = gde + dqk[S:] + nn((dat * (k2t() * rr)).astype(BF16), R.qbd[g])
        gwide = jnp.where(diag, tn(qb, dzb_b) + tn(kb, dzc_b), 0.0)
        fold = one_hot(iota((256, 128), 0) % HEAD == iota((256, 128), 1))
        gw_hi, gw_lo = split2(gwide)
        gsm = nn(gw_hi, fold) + nn(gw_lo, fold)
        wgrad_small.append(
            gsm - jnp.where(iota((256, 128), 1) < HEAD, jnp.sum(gsm, axis=-1, keepdims=True) * (1.0 / HEAD), 0.0)
        )
        dl = drate * rl * (1.0 - rl * HEAD)
        dlx = jnp.where(jrow == RATE0 + 4 * g + lane_head, dl, 0.0)
        logit_acc += nt(dlx.astype(BF16), tsel)
        dqb, dkb, dvb = dq.astype(BF16), dk.astype(BF16), (-gde).astype(BF16)
        for h in range(2):
            sl = slice(128 * h, 128 * h + 128)
            g3[TQ + 2 * g + h] = nn(x1t, dqb[:, sl]).astype(BF16)
            g3[TK + 2 * g + h] = nn(x1t, dkb[:, sl]).astype(BF16)
        part = nt(dqb, wpair(TQ + 2 * g)) + nt(dkb, wpair(TK + 2 * g)) + nt(dvb, wpair(TV + 2 * g))
        if g == 0:
            R.ot[...] = part
        else:
            R.ot[...] += part

    last_x, last_z = reduce(LAST, "x"), reduce(LAST, "z")
    go(last_x, mid_x, mid_z, back_y)
    logit_b = logit_acc.astype(BF16)
    oc_all = R.ot[...] + tt(logit_b, small)
    R.ot[...] = oc_all
    g_bias = jnp.sum(logit_acc, axis=1, keepdims=True)
    g_rate = nt(x1t, logit_b)
    g_norm_gain = jnp.zeros((1, D), F32)
    for i in range(4):
        rows = pl.ds(32 * i, 32)
        x = R.tok[rows, :].astype(F32)
        r = lax.rsqrt(jnp.mean(x * x, axis=-1, keepdims=True) + EPS)
        g_norm_gain += jnp.sum(R.ot[rows, :] * (x * r), axis=0, keepdims=True)

    vec_rows = jnp.concatenate(
        [g_norm_gain, g_init_bias, g_inner_gain, g_inner_bias, g_post_gain, g_post_bias, g_mlp_gain, jnp.zeros((9, D), F32)], axis=0
    ).astype(BF16)
    g3[TS] = (jnp.concatenate(wgrad_small, axis=0) + g_rate + tn(vec_rows, vsel)).astype(BF16)
    go(last_z)

    bias_row = jnp.sum(jnp.where(iota((S, S), 0) == iota((S, S), 1), g_bias, 0.0), axis=0, keepdims=True)
    r8 = iota((8, 128), 0)
    R.stat[...] = jnp.where(
        r8 == 0, rate_sum, jnp.where(r8 == 1, count, jnp.where(r8 == 2, rate_max, jnp.where(r8 == 3, bias_row, 0.0)))
    )
    stats = send_all([(R.stat, R.sa.at[me.s], dev) for dev, _ in peers], R.sa.at[pl.ds(0, 15)])
    R.sa[pl.ds(me.s, 1)] = R.stat[...][None]
    for i in range(4):
        rows = pl.ds(32 * i, 32)
        x = R.tok[rows, :].astype(F32)
        r = lax.rsqrt(jnp.mean(x * x, axis=-1, keepdims=True) + EPS)
        w = x * r
        f = R.ot[rows, :] * norm_gain
        R.gtok[rows, :] = (R.hcot[rows, :] + r * (f - w * jnp.mean(f * w, axis=-1, keepdims=True))).astype(BF16)
    gtok_copy = pltpu.make_async_copy(R.gtok, gtok_any, R.lsem.at[1])
    gtok_copy.start()

    go(last_x, last_z, back_z, back_x)

    def combine(buf, n):
        total, peak = buf[0], buf[0]
        for s in range(1, n):
            total, peak = total + buf[s], jnp.maximum(peak, buf[s])
        return jnp.where(r8 == 2, peak, total)

    stats.wait_recv()
    R.sb[pl.ds(me.zx, 1)] = combine(R.sa, 16)[None]
    stats2 = send_all([(R.sb.at[me.zx], R.sb.at[me.zx], me.far(*p)) for p in FARS], R.sb.at[pl.ds(0, 7)])
    for _ in range(2):
        go(last_x, last_z, mid_x, mid_z, back_y, back_z, back_x)
    finish(mid_x, mid_z, back_y, back_z, back_x)

    def owners(waves, pack, land_):
        i = 0
        for w in waves:
            for t in w.mine(me.c, me.xl, me.y):
                stf[...] = g4[t, me.z, me.xh].astype(F32)
                for s in range(16):
                    pkf[s, pl.ds(6 * i, 6), :] = stf[pl.ds(6 * s, 6), :]
                i += 1
        for s in range(16):
            pack[s] = pkf[s, 0 : pack.shape[1], :].astype(BF16)
        group = send_all([(pack.at[slot], land_.at[me.s], dev) for dev, slot in peers], land_.at[pl.ds(0, 15)])
        land_[pl.ds(me.s, 1)] = pack[pl.ds(me.s, 1)]
        return group

    early = owners(EARLY, R.pk_a, R.rv_a)
    stats2.wait_recv()
    R.stat_sum[...] = combine(R.sb, 8)
    stat_copy = pltpu.make_async_copy(R.stat_sum, stat_any, R.lsem.at[2])
    stat_copy.start()
    finish(last_x, last_z)
    late = owners(LATE, R.pk_b, R.rv_b)
    early.wait_recv()
    raw_a_copy = pltpu.make_async_copy(R.rv_a, raw_a, R.lsem.at[3])
    raw_a_copy.start()
    late.wait_recv()
    raw_b_copy = pltpu.make_async_copy(R.rv_b, raw_b, R.lsem.at[4])
    raw_b_copy.start()
    for cp in (mc_copy, n2_copy, t_copy, o_copy, stats, stats2, early, late):
        cp.wait_send()
    for cp in (out_copy, gtok_copy, stat_copy, raw_a_copy, raw_b_copy):
        cp.wait()


def step(lens, *arrays):
    anym = pl.BlockSpec(memory_space=pl.ANY)
    sd = jax.ShapeDtypeStruct
    return pl.pallas_call(
        step_kernel,
        out_shape=(
            sd((S, D), BF16), sd((S, D), BF16), sd((16, rows_of(EARLY), 128), BF16), sd((16, rows_of(LATE), 128), BF16),
            sd((8, 128), F32),
        ),
        in_specs=[pl.BlockSpec(memory_space=pltpu.SMEM)] + [anym] * len(INPUTS),
        out_specs=(anym,) * 5,
        scratch_shapes=list(SCRATCH.values()),
        compiler_params=pltpu.CompilerParams(collective_id=0, has_side_effects=True, vmem_limit_bytes=60 * 2**20),
        name="step",
    )(lens, *arrays)


def finish_kernel(raw_a, raw_b, stat, out_in, gtok_in, *outs):
    (out, gtok, g_norm, gq, gk, gv, g_rate, g_brate, g_init, g_ib, g_ig, g_ibias, g_pg, g_pb, go, g_mg, gg, gu, gd,
     r_mean, r_max, early, late) = outs
    out[...] = out_in[...]
    gtok[...] = gtok_in[...]
    mats = (gq, gk, gv, go, gg, gu, gd)
    for s in range(16):
        early[s] = raw_a[s].astype(F32)
        late[s] = raw_b[s].astype(F32)
    for h in range(2):
        for xl in range(2):
            counts = [0, 0]
            for w in BACK_WAVES:
                kind = int(w in LATE)
                pkf = (early, late)[kind]
                for n in range(w.per):
                    i = counts[kind]
                    counts[kind] += 1
                    for y in range(4 if n >= w.nx + w.nz else 1):
                        where = tile_source(w, h, w.mine(h, xl, y)[n])
                        if where is None:
                            continue
                        if n < w.nx + w.nz:
                            x = [pkf[h * 8 + xl * 4 + y_, pl.ds(6 * i, 6), :] for y_ in range(4)]
                            val = (x[0] + x[1]) + (x[2] + x[3])
                        else:
                            val = pkf[h * 8 + xl * 4 + y, pl.ds(6 * i, 6), :]
                        a, col = where
                        if a < A_S:
                            mats[a][:, 128 * col : 128 * col + 128] = val
                        else:
                            g_init[...] = val[:, :HEAD]
                            g_rate[...] = val[:, RATE0 : RATE0 + HEADS]
                            vt = val.T
                            for n_, ref in enumerate((g_norm, g_ib, g_ig, g_ibias, g_pg, g_pb, g_mg)):
                                ref[...] = vt[VEC0 + n_ : VEC0 + n_ + 1, :]
    st = stat[...]
    g_brate[...] = st[3:4, RATE0 : RATE0 + HEADS]
    r_mean[...] = st[0:1, 0:1] / st[1:2, 0:1]
    r_max[...] = st[2:3, 0:1]


def finish_call(raw_a, raw_b, stat, out, gtok):
    vm = pl.BlockSpec(memory_space=pltpu.VMEM)
    sd = jax.ShapeDtypeStruct
    row = sd((1, 6), F32)
    m768, m2048 = sd((6, 768), F32), sd((6, FF), F32)
    shapes = (
        sd((S, D), BF16), sd((S, D), BF16), row, m768, m768, m768, sd((6, HEADS), F32), sd((1, HEADS), F32),
        sd((6, HEAD), F32), row, row, row, row, row, m768, row, m2048, m2048, m2048, sd((1, 1), F32), sd((1, 1), F32),
    )
    return pl.pallas_call(
        finish_kernel, out_shape=shapes, in_specs=[vm] * 5, out_specs=(vm,) * 21,
        scratch_shapes=[f32(16, rows_of(EARLY), 128), f32(16, rows_of(LATE), 128)], name="finish",
    )(raw_a, raw_b, stat, out, gtok)


def per_device(
    tokens, cotangent, seq_lengths, norm_gain, weight_query, weight_key, weight_value, weight_rate, bias_rate,
    init_weight, init_bias, inner_gain, inner_bias, post_gain, post_bias, weight_out, mlp_gain, weight_gate, weight_up,
    weight_down,
):
    rows = (norm_gain, init_bias, inner_gain, inner_bias, post_gain, post_bias, mlp_gain)
    out, gtok, raw_a, raw_b, stat = step(
        seq_lengths, *[r.reshape(1, -1) for r in rows + (bias_rate,)], tokens, cotangent, weight_query, weight_key, weight_value, weight_out, weight_gate, weight_up,
        weight_down, init_weight, weight_rate,
    )
    res = list(finish_call(raw_a, raw_b, stat, out, gtok))
    for i in (2, 9, 10, 11, 12, 13, 15):
        res[i] = res[i].reshape(6)
    res[7] = res[7].reshape(HEADS)
    res[19], res[20] = res[19].reshape(()), res[20].reshape(())
    return tuple(res)


def solution(mesh):
    both = ("dp", "sub")
    mat, vec, rep = P(both, None), P(both), P()
    return jax.shard_map(
        per_device,
        mesh=mesh,
        in_specs=(mat, mat, mat, vec, mat, mat, mat, mat, rep, mat, vec, vec, vec, vec, vec, mat, vec, mat, mat, mat),
        out_specs=(mat, mat, vec, mat, mat, mat, mat, rep, mat, vec, vec, vec, vec, vec, mat, vec, mat, mat, mat, rep, rep),
        check_vma=False,
    )
```
